256 devices in a mesh: sfc: 128 (over z, y, x), lev: 2 (over core).
Axes of the slice: x: 4, y: 4, z: 8, core: 2. Of those that a mesh axis runs over, the one named last changes fastest.
Arguments:
- tracers: float32 [8, 32, 16, 32768], P(None, 'lev', None, 'sfc'), may hold values from -6 to 6
- layer_mass: float32 [32, 16, 32768], P('lev', None, 'sfc'), may hold values from 0.5 to 2
- layer_mass_next: float32 [32, 16, 32768], P('lev', None, 'sfc'), may hold values from 0.5 to 2
- wind: float32 [2, 32, 16, 32768], P(None, 'lev', None, 'sfc'), may hold values from -4 to 4
- spheremp: float32 [16, 32768], P(None, 'sfc'), may hold values from 0.25 to 4
- inverse_mass: float32 [16, 32768], P(None, 'sfc'), may hold values from 0.15 to 0.6
- rec_peer: int32 [8, 32768], P(None, 'sfc'), may hold values from -1 to 127, as said below
- rec_slot: int32 [8, 32768], P(None, 'sfc'), may hold values from 0 to 1023, as said below
- rec_flip: int32 [8, 32768], P(None, 'sfc'), may hold values from 0 to 1, as said below
- publish_list: int32 [8192], P('sfc'), may hold values from -1 to 1023, as said below
- column_slot_table: int32 [4, 32768], P(None, 'sfc'), may hold values from 0 to 163839, as said below
Outputs:
- tracer_mass: float32 [8, 32, 16, 32768], P(None, 'lev', None, 'sfc')
- physics_mix: float32 [8, 32, 163840], P(None, None, ('sfc', 'lev'))
- sigma_mid: float32 [32, 163840], P(None, ('sfc', 'lev'))
The draws below stay inside these ranges and needn't reach their ends.
Inputs may be any that keep to these rules, and one draw needn't show every extreme that they name: `rec_peer`: records 0 to 3 name the element across sides 0 to 3, records 4 to 7 the element diagonally across corners 0, 3, 12, 15 (sharing only that point); -1 where there is none. A peer differs from the element's own device by 0, 1, -1, 32, -32, 33, 31, 1 - 32 or -1 - 32. No device has more than 46 records naming one other device, and some device has exactly 46. Every point shared by elements is read by each of them from each other. `rec_slot`: A remote record's entry in the peer's publish list is not -1 and names the side that faces the record's element (for corners, a side holding the shared point); a local record's value is 4 n + s2. Records with no peer hold 0. `rec_flip`: side records: 1 where the neighbour's side runs the other way. Corner records: 0 if the shared point is position 0 of the named side, 1 if it is position 3. `publish_list`: each device's 64 entries are distinct values 4 n + s of its own elements, or -1 anywhere in the list; some device has no -1. `column_slot_table`: all distinct. The columns of one device's elements name exactly 8 slots in each block of 1280 consecutive slots.
All inputs are finite; a program needn't handle non-finite values.
Results may differ from the reference program's by a relative error of at most 0.0003.
Values sent between devices are 32-bit elements; how exact they have to be, the bound alone decides.
No kernel may reach another device: no remote copies, remote signals or barrier semaphores. Data moves between devices by JAX's collectives and lax.ppermute only.
A program may use at most 128 MiB of HBM per device.

```python
import math
import jax
import jax.numpy as jnp
import numpy as np
from jax import lax

NPTS = 16
NPG = 4
TRACER_SUBSET = 8
LAYER_COUNT = 32
ELEM_DEV = 256
TILE_H = 16
DEV_ROWS = 4
TILE_W = 16
DEV_COLS = 32
NELEM = 32768
PUB = 64
CAPC = 8
SLOT_TOTAL = 163840
N_SFC = 128


def edge_topology(key):
    base_key = jax.random.fold_in(key, 7)
    key_rows, key_perm, key_score, key_shuffle = jax.random.split(base_key, 4)
    mirror_row = jax.random.randint(key_rows, (DEV_ROWS,), 0, 2)
    local_perm = jax.vmap(lambda k: jax.random.permutation(k, ELEM_DEV))(jax.random.split(key_perm, N_SFC))
    span_x = DEV_COLS * TILE_W
    span_y = DEV_ROWS * TILE_H
    grid_y, grid_x = jnp.meshgrid(jnp.arange(span_y), jnp.arange(span_x), indexing='ij')

    def locate(coord_x, coord_y):
        inside = (coord_x >= 0) & (coord_x < span_x) & (coord_y >= 0) & (coord_y < span_y)
        clip_x = jnp.clip(coord_x, 0, span_x - 1)
        clip_y = jnp.clip(coord_y, 0, span_y - 1)
        device = clip_y // TILE_H * DEV_COLS + clip_x // TILE_W
        place = clip_y % TILE_H * TILE_W + clip_x % TILE_W
        return (inside, device, local_perm[device, place], mirror_row[clip_y // TILE_H])
    unused, own_device, own_slot, own_mirror = locate(grid_x, grid_y)
    side_records = []
    flags = jnp.zeros((N_SFC, 4 * ELEM_DEV), jnp.int32)
    for side in range(4):
        if side == 0:
            step_x, step_y = (jnp.zeros_like(grid_x), -1)
        elif side == 2:
            step_x, step_y = (jnp.zeros_like(grid_x), 1)
        elif side == 1:
            step_x, step_y = (1 - 2 * own_mirror, 0)
        else:
            step_x, step_y = (2 * own_mirror - 1, 0)
        inside, near_device, near_slot, near_mirror = locate(grid_x + step_x, grid_y + step_y)
        if side == 0:
            near_side = jnp.full_like(grid_x, 2)
            flip = jnp.bitwise_xor(own_mirror, near_mirror)
        elif side == 2:
            near_side = jnp.zeros_like(grid_x)
            flip = jnp.bitwise_xor(own_mirror, near_mirror)
        else:
            near_side = jnp.where(step_x == 1, 3 - 2 * near_mirror, 1 + 2 * near_mirror)
            flip = jnp.zeros_like(grid_x)
        outward = inside & (near_device != own_device)
        flags = flags.at[own_device, own_slot * 4 + side].max(outward.astype(jnp.int32))
        side_records.append((inside, near_device, near_slot * 4 + near_side, flip))
    scores = jax.vmap(lambda k: jax.random.permutation(k, 4 * ELEM_DEV))(jax.random.split(key_score, N_SFC))
    keyed = jnp.where(flags == 1, scores, scores + 4 * ELEM_DEV)
    ordered = jnp.argsort(keyed, axis=1, stable=True)[:, :PUB].astype(jnp.int32)
    listed = jnp.where(jnp.take_along_axis(flags, ordered, axis=1) == 1, ordered, -1)
    shuffle = jax.vmap(lambda k: jax.random.permutation(k, PUB))(jax.random.split(key_shuffle, N_SFC))
    listed = jnp.take_along_axis(listed, shuffle, axis=1)
    device_rows = jnp.broadcast_to(jnp.arange(N_SFC)[:, None], (N_SFC, PUB))
    position_of = jnp.zeros((N_SFC, 4 * ELEM_DEV), jnp.int32).at[device_rows, jnp.where(listed >= 0, listed, 4 * ELEM_DEV)].set(jnp.broadcast_to(jnp.arange(PUB, dtype=jnp.int32)[None], (N_SFC, PUB)), mode='drop')
    corner_records = []
    for corner_i, corner_j in [(0, 0), (3, 0), (0, 3), (3, 3)]:
        rightward = own_mirror == (0 if corner_i == 3 else 1)
        step_x = jnp.where(rightward, 1, -1)
        step_y = 1 if corner_j == 3 else -1
        inside, diag_device, diag_slot, diag_mirror = locate(grid_x + step_x, grid_y + step_y)
        unused_a, beside_device, unused_b, unused_c = locate(grid_x + step_x, grid_y)
        horizontal = (diag_device == own_device) | (beside_device != diag_device)
        phys_i = jnp.where(step_x > 0, 0, 3)
        phys_j = 0 if step_y > 0 else 3
        h_side = 0 if step_y > 0 else 2
        h_position = jnp.where(diag_mirror == 0, phys_i, 3 - phys_i)
        v_side = jnp.where(step_x > 0, 3 - 2 * diag_mirror, 1 + 2 * diag_mirror)
        chosen_side = jnp.where(horizontal, h_side, v_side)
        position = jnp.where(horizontal, h_position, phys_j)
        corner_records.append((inside, diag_device, diag_slot * 4 + chosen_side, position // 3))
    global_index = (own_device * ELEM_DEV + own_slot).reshape(-1)
    peers, slots, flips = ([], [], [])
    for inside, device, code, flip in side_records + corner_records:
        slot_value = jnp.where(device == own_device, code, position_of[device, code])
        peers.append(jnp.where(inside, device, -1).reshape(-1))
        slots.append(jnp.where(inside, slot_value, 0).reshape(-1))
        flips.append(jnp.where(inside, flip, 0).reshape(-1))
    peer_all = jnp.zeros((8, NELEM), jnp.int32).at[:, global_index].set(jnp.stack(peers).astype(jnp.int32))
    slot_all = jnp.zeros((8, NELEM), jnp.int32).at[:, global_index].set(jnp.stack(slots).astype(jnp.int32))
    flip_all = jnp.zeros((8, NELEM), jnp.int32).at[:, global_index].set(jnp.stack(flips).astype(jnp.int32))
    return (peer_all, slot_all, flip_all, listed.reshape(-1).astype(jnp.int32))


def draw_rec_peer(key, part):
    return edge_topology(key)[0]


def draw_rec_slot(key, part):
    return edge_topology(key)[1]


def draw_rec_flip(key, part):
    return edge_topology(key)[2]


def draw_publish_list(key, part):
    return edge_topology(key)[3]


def draw_column_slot_table(key, part):
    base_key = jax.random.fold_in(key, 13)
    key_rank, key_place = jax.random.split(base_key, 2)
    group_width = SLOT_TOTAL // N_SFC
    ranks = jax.vmap(lambda k: jax.random.permutation(k, NPG * ELEM_DEV))(jax.random.split(key_rank, N_SFC))
    group = ranks // CAPC
    within_rank = ranks % CAPC
    place_perm = jax.vmap(lambda k: jax.random.permutation(k, group_width))(jax.random.split(key_place, N_SFC))
    source = jnp.arange(N_SFC)[:, None]
    slot_value = group * group_width + place_perm[group, source * CAPC + within_rank]
    return slot_value.reshape(N_SFC, NPG, ELEM_DEV).transpose(1, 0, 2).reshape(NPG, NELEM).astype(jnp.int32)


def block_scale(own_key, extent, shards, least, high):
    def one(dim, blocks):
        heights = jax.random.uniform(jax.random.fold_in(jax.random.fold_in(own_key, 6), dim), (blocks,), jnp.float32, least / len(shards), high / len(shards))
        return jnp.repeat(jnp.exp(heights), extent[dim] // blocks).reshape((-1,) + (1,) * (len(extent) - dim - 1))

    level = one(*shards[0])
    for cut in shards[1:]:
        level = level * one(*cut)
    return level


def bell_draw(stream_key, shape, spread, limit, shards=(), kind=jnp.bfloat16):
    factor_of = block_scale(stream_key, shape, shards, -0.22, 0.18) if shards else 1.0
    values = jax.random.normal(stream_key, shape, jnp.float32) * spread * factor_of
    return jnp.minimum(jnp.maximum(values, -limit), limit).astype(kind)


def setup_inputs(seed: int = 0) -> dict:
    keys = jax.random.split(jax.random.key(seed), 12)
    return {
        "tracers": bell_draw(keys[0], (TRACER_SUBSET, LAYER_COUNT, NPTS, NELEM), 1.0, 6.0, ((1, 2), (3, 128)), jnp.float32),
        "layer_mass": jnp.clip(jnp.exp(math.log(2.0) - 1.3862944 * jax.random.uniform(keys[1], (LAYER_COUNT, NPTS, NELEM), jnp.float32) ** block_scale(keys[1], (LAYER_COUNT, NPTS, NELEM), ((0, 2), (2, 128)), -0.2, 0.2)), 0.5, 2.0),
        "layer_mass_next": jnp.clip(jnp.exp(math.log(2.0) - 1.3862944 * jax.random.uniform(keys[2], (LAYER_COUNT, NPTS, NELEM), jnp.float32) ** block_scale(keys[2], (LAYER_COUNT, NPTS, NELEM), ((0, 2), (2, 128)), -0.2, 0.2)), 0.5, 2.0),
        "wind": bell_draw(keys[3], (2, LAYER_COUNT, NPTS, NELEM), 1.0, 4.0, ((1, 2), (3, 128)), jnp.float32),
        "spheremp": jnp.clip(jnp.exp(math.log(4.0) - 2.7725887 * jax.random.uniform(keys[4], (NPTS, NELEM), jnp.float32) ** block_scale(keys[4], (NPTS, NELEM), ((1, 128),), -0.2, 0.2)), 0.25, 4.0),
        "inverse_mass": jnp.clip(jnp.exp(math.log(0.6) - 1.3862944 * jax.random.uniform(keys[5], (NPTS, NELEM), jnp.float32) ** block_scale(keys[5], (NPTS, NELEM), ((1, 128),), -0.2, 0.2)), 0.15, 0.6),
        "rec_peer": draw_rec_peer(jax.random.fold_in(keys[11], 71), 0),
        "rec_slot": draw_rec_slot(jax.random.fold_in(keys[11], 71), 0),
        "rec_flip": draw_rec_flip(jax.random.fold_in(keys[11], 71), 0),
        "publish_list": draw_publish_list(jax.random.fold_in(keys[11], 71), 0),
        "column_slot_table": draw_column_slot_table(jax.random.fold_in(keys[11], 71), 0),
    }


def lagrange_derivative():
    gll_points = np.array([-1.0, -1.0 / np.sqrt(5.0), 1.0 / np.sqrt(5.0), 1.0])
    barycentric = np.array([1.0 / np.prod([gll_points[source] - gll_points[middle] for middle in range(4) if middle != source]) for source in range(4)])
    derivative = np.zeros((4, 4))
    for target in range(4):
        for source in range(4):
            if target != source:
                derivative[target, source] = barycentric[source] / barycentric[target] / (gll_points[target] - gll_points[source])
        derivative[target, target] = -np.sum(derivative[target])
    return derivative

def stacked_derivative():
    lagrange = lagrange_derivative()
    return np.stack([np.kron(np.eye(4), lagrange), np.kron(lagrange, np.eye(4))], axis=1)

def quadrant_table():
    table = np.zeros((4, 16))
    for point in range(16):
        table[2 * (point // 4 // 2) + point % 4 // 2, point] = 1.0
    return table
SIDE_POINTS = np.array([[0, 1, 2, 3], [3, 7, 11, 15], [12, 13, 14, 15], [0, 4, 8, 12]])
CORNER_POINTS = [0, 3, 12, 15]
TIME_STEP = 0.05
TOP_PRESSURE = 1.0
MIXING_RATE = 0.8

def side_table(field):
    sides = field[:, SIDE_POINTS]
    return jnp.transpose(sides, (0, 2, 3, 1)).reshape(field.shape[0], 4, -1)

def record_sources(rec_peer, rec_slot, publish_list):
    owner = (jnp.arange(NELEM) // ELEM_DEV).astype(jnp.int32)
    valid = rec_peer >= 0
    peer_clip = jnp.clip(rec_peer, 0, N_SFC - 1).astype(jnp.int32)
    remote = valid & (peer_clip != owner[None, :])
    published = publish_list[(peer_clip * PUB + jnp.clip(rec_slot, 0, PUB - 1)).astype(jnp.int32)]
    local_code = jnp.clip(rec_slot, 0, 4 * ELEM_DEV - 1)
    code = jnp.where(remote, jnp.maximum(published, 0), local_code)
    return ((peer_clip * (4 * ELEM_DEV) + code).astype(jnp.int32), valid)

def assemble(field, sources, valid, rec_flip):
    table = side_table(field)
    total = field
    for record in range(8):
        values = table[:, :, sources[record]]
        values = jnp.where(rec_flip[record] == 1, values[:, ::-1], values)
        values = jnp.where(valid[record], values, jnp.zeros_like(values))
        if record < 4:
            total = total.at[:, SIDE_POINTS[record]].add(values)
        else:
            total = total.at[:, CORNER_POINTS[record - 4]].add(values[:, 0])
    return total

def reference(tracers, layer_mass, layer_mass_next, wind, spheremp, inverse_mass, rec_peer, rec_slot, rec_flip, publish_list, column_slot_table):
    highest = lax.Precision.HIGHEST
    sources, valid = record_sources(rec_peer, rec_slot, publish_list)
    derivative = jnp.asarray(stacked_derivative(), dtype=tracers.dtype)
    quadrant = jnp.asarray(quadrant_table(), dtype=tracers.dtype)
    mass_den = jnp.einsum('ck,lke->lce', quadrant, spheremp[None] * layer_mass_next, precision=highest)
    area_pg = jnp.einsum('ck,ke->ce', quadrant, spheremp, precision=highest)
    thickness_columns = mass_den / area_pg[None]

    def one_tracer(tracer):
        mass = layer_mass * tracer
        fluxes = wind * mass[None]
        divergence = jnp.einsum('kaq,alqe->lke', derivative, fluxes, precision=highest)
        mass_new = mass - TIME_STEP * divergence
        assembled = assemble(spheremp[None] * mass_new, sources, valid, rec_flip)
        mass_out = inverse_mass[None] * assembled
        mix_num = jnp.einsum('ck,lke->lce', quadrant, spheremp[None] * mass_out, precision=highest)
        return (mass_out, mix_num / mass_den)
    tracer_mass, mixing_ratio_columns = lax.map(one_tracer, tracers)
    live_flags = jnp.zeros((SLOT_TOTAL,), tracers.dtype).at[column_slot_table].set(1.0)
    physics_mixing_ratio = jnp.zeros((TRACER_SUBSET, LAYER_COUNT, SLOT_TOTAL), tracers.dtype).at[:, :, column_slot_table].set(mixing_ratio_columns)
    physics_layer_thickness = jnp.zeros((LAYER_COUNT, SLOT_TOTAL), tracers.dtype).at[:, column_slot_table].set(thickness_columns)
    column_sum = lax.optimization_barrier(jnp.sum(physics_layer_thickness, axis=0))
    above = jnp.cumsum(physics_layer_thickness, axis=0) - physics_layer_thickness
    sigma_mid = live_flags[None] * (TOP_PRESSURE + above + 0.5 * physics_layer_thickness) / (TOP_PRESSURE + column_sum)[None]
    mean_mix = lax.optimization_barrier(jnp.sum(physics_layer_thickness[None] * physics_mixing_ratio, axis=1)) / (column_sum + 1.0 - live_flags)[None]
    physics_mix = physics_mixing_ratio + MIXING_RATE * sigma_mid[None] * (mean_mix[:, None] - physics_mixing_ratio)
    return (tracer_mass, physics_mix, sigma_mid)
```

```python
import functools

import jax
import jax.numpy as jnp
import numpy as np
from jax import lax
from jax.experimental import pallas as pl
from jax.experimental.pallas import tpu as pltpu
from jax.sharding import PartitionSpec as P

F32 = jnp.float32
BF16 = jnp.bfloat16
NPG = 4
DEV_ROWS = 4
SIDE_POINTS = [[0, 1, 2, 3], [3, 7, 11, 15], [12, 13, 14, 15], [0, 4, 8, 12]]
CORNER_POINTS = [0, 3, 12, 15]
CORNER_SIDES = [[(0, 0), (3, 0)], [(0, 3), (1, 0)], [(2, 0), (3, 3)], [(1, 3), (2, 3)]]
EDGE_SLOTS = [(s, m) for s in range(4) for m in (1, 2)]
TIME_STEP = 0.05
TOP_PRESSURE = 1.0
MIXING_RATE = 0.8
PER_SIDE = 16
ROWS = 10


def lagrange_derivative():
    gll_points = np.array([-1.0, -1.0 / np.sqrt(5.0), 1.0 / np.sqrt(5.0), 1.0])
    barycentric = np.array(
        [
            1.0
            / np.prod(
                [gll_points[source] - gll_points[middle] for middle in range(4) if middle != source]
            )
            for source in range(4)
        ]
    )
    derivative = np.zeros((4, 4))
    for target in range(4):
        for source in range(4):
            if target != source:
                derivative[target, source] = (
                    barycentric[source]
                    / barycentric[target]
                    / (gll_points[target] - gll_points[source])
                )
        derivative[target, target] = -np.sum(derivative[target])
    return derivative


def iota(shape, dim):
    return lax.broadcasted_iota(jnp.int32, shape, dim)


def hot(mask):
    return jnp.where(mask, 1.0, 0.0).astype(BF16)


def split(x, axis=0):
    high = x.astype(BF16)
    low = (x - high.astype(F32)).astype(BF16)
    return jnp.concatenate([high, low], axis=axis)


def dot_nn(a, b):
    return lax.dot_general(a, b, (((1,), (0,)), ((), ())), preferred_element_type=F32)


def dot_nt(a, b):
    return lax.dot_general(a, b, (((1,), (1,)), ((), ())), preferred_element_type=F32)


def wide(ref, first=0):
    return jnp.concatenate([ref[first + s : first + s + 1, :] for s in range(4)], axis=1)


def facing(peer, own, block_cols):
    ahead = peer - own
    code = jnp.full_like(peer, -1)
    for number, offset in enumerate((1, -1, block_cols, -block_cols)):
        code = jnp.where(ahead == offset, number, code)
    return jnp.where(peer >= 0, code, -1)


def ranks(direction, entry):
    count = direction.shape[1]
    code = jnp.where(direction >= 0, direction * 64 + entry, -1)
    found = jnp.where(iota((256, count), 0) == code, 1.0, 0.0)
    present = jnp.max(found, axis=1, keepdims=True)
    row, col = iota((256, 256), 0), iota((256, 256), 1)
    before = hot((col < row) & (col // 64 == row // 64))
    below = dot_nn(before, jnp.broadcast_to(present, (256, 128)).astype(BF16))
    rank = jnp.sum(found * below[:, :1], axis=0, keepdims=True)
    return rank.astype(jnp.int32)


def flux_kernel(block_cols, own_ref, tr_ref, lm_ref, wd_ref, sph_ref, peer_ref, slot_ref, x_ref, msg_ref, info_ref):
    half = pl.program_id(0)
    deriv = lagrange_derivative() * TIME_STEP
    levels = lm_ref.shape[0] // 16
    tracers = tr_ref.shape[0] // lm_ref.shape[0]
    elems = peer_ref.shape[1]
    lanes = tr_ref.shape[1]

    def one(t, carry):
        mass, fa, fb = [], [], []
        for k in range(16):
            tr = tr_ref[pl.ds(t * (levels * 16) + k, levels, stride=16), :]
            mk = tr * lm_ref[pl.ds(k, levels, stride=16), :]
            mass.append(mk)
            fa.append(mk * wd_ref[pl.ds(k, levels, stride=16), :])
            fb.append(mk * wd_ref[pl.ds(levels * 16 + k, levels, stride=16), :])
        for k in range(16):
            j, i = k // 4, k % 4
            value = mass[k]
            for other in range(4):
                if abs(deriv[i, other]) > 1e-12:
                    value = value - deriv[i, other] * fa[4 * j + other]
                if abs(deriv[j, other]) > 1e-12:
                    value = value - deriv[j, other] * fb[4 * other + i]
            x_ref[k, pl.ds(pl.multiple_of(t * levels, levels), levels), :] = value * sph_ref[k : k + 1, :]
        return carry

    lax.fori_loop(0, tracers, one, 0)

    @pl.when(half == 0)
    def _():
        direction = facing(wide(peer_ref), own_ref[0], block_cols)
        rank = ranks(direction, jnp.clip(wide(slot_ref), 0, 63))
        usable = (direction >= 0) & (rank < PER_SIDE)
        base = jnp.where(usable, direction * 64 + rank, -1000)
        info_ref[...] = jnp.broadcast_to(base, info_ref.shape)
        msg_ref[...] = jnp.zeros_like(msg_ref)

    lane = iota((256, lanes), 0)
    total = None
    for group in [[pair] for pair in EDGE_SLOTS] + CORNER_SIDES:
        pick = None
        for s, m in group:
            base = info_ref[:1, pl.ds(pl.multiple_of(s * elems + half * lanes, lanes), lanes)]
            here = lane == base + m * PER_SIDE
            pick = here if pick is None else pick | here
        s, m = group[0]
        part = dot_nt(split(x_ref[SIDE_POINTS[s][m]]), hot(pick))
        total = part if total is None else total + part
    fields = total.shape[0] // 2
    msg_ref[...] += total[:fields] + total[fields:]


def local_kernel(block_cols, own_ref, x_ref, peer_ref, slot_ref, flip_ref, pub_ref, info_ref, xd_ref, far_ref, mid_ref):
    own = own_ref[0]
    elems = peer_ref.shape[1]
    fields = x_ref.shape[1]
    sides = 4 * elems
    peer, slot, flip = wide(peer_ref), wide(slot_ref), wide(flip_ref)
    at = iota((1, sides), 1)
    own_code = 4 * (at % elems) + at // elems
    match = jnp.where(pub_ref[...] == own_code, 1.0, 0.0)
    place = jnp.sum(match * iota((64, sides), 0).astype(F32), axis=0, keepdims=True).astype(jnp.int32)
    direction = facing(peer, own, block_cols)
    rank = ranks(direction, place)
    usable = (direction >= 0) & (rank < PER_SIDE)
    start = jnp.where(direction == 0, 64, jnp.where(direction == 1, 0, jnp.where(direction == 2, 192, 128)))
    recv = jnp.where(usable, start + rank, -1000)

    def arrive(s, m):
        cols = slice(s * elems, (s + 1) * elems)
        turned = jnp.where(flip[:, cols] == 1, 3 - m, m)
        return recv[:, cols] + turned * PER_SIDE

    lane = iota((256, elems), 0)
    corner_far = []
    for c in range(4):
        (sa, ma), (sb, mb) = CORNER_SIDES[c]
        corner_far.append(hot((lane == arrive(sa, ma)) | (lane == arrive(sb, mb))))
    corner_far = jnp.concatenate(corner_far, axis=1)
    for number, (s, m) in enumerate(EDGE_SLOTS):
        far_ref[4 + number] = hot(lane == arrive(s, m))
    base = info_ref[:1, :]
    second = jnp.where(base >= 128, base - 128, -1000)
    lane128 = iota((128, elems), 0)
    sent = []
    for c in range(4):
        pick = None
        for s, m in CORNER_SIDES[c]:
            here = lane128 == second[:, s * elems : (s + 1) * elems] + m * PER_SIDE
            pick = here if pick is None else pick | here
        sent.append(hot(pick))
    mid_ref[...] = dot_nt(corner_far[:128], jnp.concatenate(sent, axis=1)).astype(BF16)

    local = peer == own
    slot_c = jnp.clip(slot, 0, 4 * elems - 1)
    near = jnp.where(local, slot_c % 4 * elems + slot_c // 4, -1)

    def corner_source(code, end, ok):
        side = code % 4
        corner = jnp.where(side == 1, 1, jnp.where(side == 2, 2, 0)) + end * jnp.where(side % 2 == 1, 2, 1)
        return jnp.where(ok, corner * elems + code // 4, -1)

    cpeer, cslot, cflip = wide(peer_ref, 4), wide(slot_ref, 4), wide(flip_ref, 4)
    third = corner_source(jnp.clip(cslot, 0, 4 * elems - 1), cflip, cpeer == own)
    source = iota((sides, elems), 0)
    corners = jnp.concatenate([x_ref[p] for p in CORNER_POINTS], axis=1)
    corners_hl = split(corners)
    lhs = jnp.concatenate([corners_hl, corner_far], axis=0)
    for c in range(4):
        cols = slice(c * elems, (c + 1) * elems)
        weight = jnp.where(source == third[:, cols], 1.0, 0.0)
        for s, m in CORNER_SIDES[c]:
            own_cols = slice(s * elems, (s + 1) * elems)
            end = jnp.where(flip[:, own_cols] == 1, 1 - m // 3, m // 3)
            code = corner_source(slot_c[:, own_cols], end, local[:, own_cols])
            weight = weight + jnp.where(source == code, 1.0, 0.0)
        got = dot_nn(lhs, weight.astype(BF16))
        xd_ref[CORNER_POINTS[c]] = corners[:, cols] + got[:fields] + got[fields : 2 * fields]
        far_ref[c] = corner_far[:, cols] + got[2 * fields :].astype(BF16)
    inner = []
    for m in (1, 2):
        inner.append(split(jnp.concatenate([x_ref[SIDE_POINTS[s][m]] for s in range(4)], axis=1)))
    inner = jnp.concatenate(inner, axis=0)
    for s in range(4):
        cols = slice(s * elems, (s + 1) * elems)
        got = dot_nn(inner, hot(source == near[:, cols]))
        one = got[:fields] + got[fields : 2 * fields]
        two = got[2 * fields : 3 * fields] + got[3 * fields :]
        turned = flip[:, cols] == 1
        for m, mine, swapped in ((1, one, two), (2, two, one)):
            p = SIDE_POINTS[s][m]
            xd_ref[p] = x_ref[p] + jnp.where(turned, swapped, mine)
    for p in (5, 6, 9, 10):
        xd_ref[p] = x_ref[p]


def merge(odd, a, b):
    low = iota(a.shape, 1) < 64
    lower = jnp.where(odd == 1, a, b)
    upper = jnp.where(odd == 1, b, a)
    return jnp.where(low, lower, upper)


def middle_kernel(odd_ref, a_ref, b_ref, msg_ref, mid_ref, got_ref, out_ref):
    got = merge(odd_ref[0], a_ref[...], b_ref[...])
    got_ref[...] = got
    fields = got.shape[0]
    add = dot_nn(split(got), mid_ref[...])
    out_ref[...] = msg_ref[:, 128:] + add[:fields] + add[fields:]


def sort_kernel(group_width, slot_ref, lmn_a_ref, lmn_b_ref, sph_ref, order_ref, rden_ref, rows_ref):
    elems = sph_ref.shape[1]
    levels = lmn_a_ref.shape[0] // 16
    sph = sph_ref[...]
    thicks = []
    for c in range(4):
        den, area = None, None
        for k in range(16):
            if 2 * (k // 8) + k % 4 // 2 != c:
                continue
            weight = sph[k : k + 1, :]
            term = [ref[pl.ds(k, levels, stride=16), :] for ref in (lmn_a_ref, lmn_b_ref)]
            term = jnp.concatenate(term, axis=1) * weight
            den = term if den is None else den + term
            area = weight if area is None else area + weight
        rden_ref[c] = 1.0 / den
        thicks.append(den / area)
    thick = jnp.concatenate(thicks, axis=1)
    total = 4 * elems
    slot = wide(slot_ref)
    slot_f = slot.astype(F32)
    dest = jnp.floor((slot_f + 0.5) * (1.0 / group_width)).astype(jnp.int32)
    within = (slot - dest * group_width).astype(F32)
    peers = rows_ref.shape[1]
    to = jnp.where(iota((peers, total), 0) == dest, 1.0, 0.0)
    to_b = to.astype(BF16)
    upto = hot(iota((128, 128), 0) < iota((128, 128), 1))
    base = jnp.zeros((peers, 1), F32)
    parts = []
    for block in range(total // 128):
        cols = slice(block * 128, block * 128 + 128)
        parts.append(dot_nn(to_b[:, cols], upto) + base)
        base = base + jnp.sum(to[:, cols], axis=1, keepdims=True)
    rank = jnp.sum(to * jnp.concatenate(parts, axis=1), axis=0, keepdims=True).astype(jnp.int32)
    key = dest * 8 + rank
    for block in range(total // 128):
        order_ref[block * 128 : block * 128 + 128, :] = hot(iota((128, total), 0) + block * 128 == key)
    at = iota((128, total), 0)
    spread = jnp.where(at // levels == rank, jnp.concatenate([thick] * (128 // levels), axis=0), 0.0)
    ids = jnp.where(at == rank, within, 0.0)
    both = jnp.concatenate([split(spread), split(ids)], axis=0)
    got = dot_nt(to_b, both)
    rows_ref[0] = got[:, :128] + got[:, 128:256]
    rows_ref[1] = got[:, 256:384] + got[:, 384:]


def finish_kernel(
    odd_ref, xd_ref, one_ref, a_ref, b_ref, far_ref, sph_ref, inv_ref, rden_ref, order_ref, rows_ref, tm_ref, out_ref, mix_ref
):
    half = pl.program_id(0)
    fields, lanes = xd_ref.shape[1], xd_ref.shape[2]
    levels = rden_ref.shape[1]
    two = merge(odd_ref[0], a_ref[...], b_ref[...])
    got = split(jnp.concatenate([one_ref[...], two], axis=1))
    number = {p: c for c, p in enumerate(CORNER_POINTS)}
    for index, (s, m) in enumerate(EDGE_SLOTS):
        number[SIDE_POINTS[s][m]] = 4 + index
    sums = [None] * 4
    for k in range(16):
        value = xd_ref[k]
        if k in number:
            far = dot_nn(got, far_ref[number[k]])
            value = value + far[:fields] + far[fields:]
        value = value * inv_ref[k : k + 1, :]
        tm_ref[pl.ds(k, fields, stride=16), :] = value
        c = 2 * (k // 8) + k % 4 // 2
        term = value * sph_ref[k : k + 1, :]
        sums[c] = term if sums[c] is None else sums[c] + term
    for c in range(4):
        mix = sums[c] * jnp.concatenate([rden_ref[c]] * (fields // levels), axis=0)
        mix_ref[:, pl.ds(pl.multiple_of(c * 2 * lanes + half * lanes, lanes), lanes)] = split(mix)

    @pl.when(half == 1)
    def _():
        mix_hl = mix_ref[...]
        peers = rows_ref.shape[1]
        chunk = 128
        for block in range(peers * 8 // chunk):
            res = dot_nt(order_ref[block * chunk : (block + 1) * chunk, :], mix_hl)
            res = res[:, :fields] + res[:, fields:]
            for d in range(chunk // 8):
                row = (block * (chunk // 8) + d) * ROWS
                out_ref[row : row + 8, :] = res[d * 8 : d * 8 + 8, :]
        out_ref[pl.ds(8, peers, stride=ROWS), :] = rows_ref[0]
        out_ref[pl.ds(9, peers, stride=ROWS), :] = rows_ref[1]


def physics_kernel(lev_ref, own_ref, par_ref, mix_ref, sig_ref):
    lev = lev_ref[0]
    total, fields = own_ref.shape
    peers = total // ROWS
    levels2, slots = sig_ref.shape
    levels = levels2 // 2
    tracers = fields // levels
    first = jnp.where(lev == 0, own_ref[...], par_ref[...])
    last = jnp.where(lev == 0, par_ref[...], own_ref[...])
    thick_own = own_ref[pl.ds(8, peers, stride=ROWS), :]
    thick_par = par_ref[pl.ds(8, peers, stride=ROWS), :]
    thick_first = jnp.where(lev == 0, thick_own, thick_par)
    thick_last = jnp.where(lev == 0, thick_par, thick_own)
    ids = own_ref[pl.ds(9, peers, stride=ROWS), :]
    at = iota((peers, total), 1)
    spread = hot(at // ROWS == iota((peers, total), 0))
    ids_t = jnp.transpose(ids)[:16, :]
    cand = dot_nn(split(ids_t), spread)
    cand = cand[:16] + cand[16:]
    spot = iota((16, total), 1) % ROWS
    key = jnp.sum(jnp.where((spot == iota((16, total), 0)) & (spot < 8), cand, 0.0), axis=0, keepdims=True)
    key = jnp.where(iota((1, total), 1) % ROWS < 8, key, -1e6).astype(jnp.int32)
    key = key - lev * slots
    spread_t = hot(iota((total, peers), 0) // ROWS == iota((total, peers), 1))
    thick_hl = jnp.concatenate([split(thick_first, axis=1), split(thick_last, axis=1)], axis=1)
    rows = dot_nn(spread_t, thick_hl)
    keep = iota((total, 128), 1) // levels == iota((total, 128), 0) % ROWS
    fold_row = iota((128, 128), 0) % levels
    fold_col = iota((128, 128), 1)
    narrow = None
    for number in range(2):
        mine = rows[:, number * 256 : number * 256 + 128] + rows[:, number * 256 + 128 : number * 256 + 256]
        mine = split(jnp.where(keep, mine, 0.0), axis=0)
        fold = hot(fold_col == fold_row + number * levels)
        part = dot_nn(mine, fold)
        part = part[:total] + part[total:]
        narrow = part if narrow is None else narrow + part
    narrow = jnp.where(iota((total, 128), 1) == levels2, 1.0, narrow)
    stack = jnp.concatenate([first, last, narrow], axis=1)
    stack = split(stack, axis=1)
    width = 2 * fields + 128
    chunk = 128
    outs = []
    for block in range(slots // chunk):
        pick = hot(iota((chunk, total), 0) + block * chunk == key)
        got = dot_nn(pick, stack)
        outs.append(jnp.transpose(got[:, :width] + got[:, width:]))
    for block in range(slots // chunk):
        got = outs[block]
        cols = slice(block * chunk, (block + 1) * chunk)
        thick = got[2 * fields : 2 * fields + levels2]
        live = got[2 * fields + levels2 : 2 * fields + levels2 + 1]
        running = jnp.zeros_like(live)
        above = []
        for level in range(levels2):
            above.append(running)
            running = running + thick[level : level + 1]
        above = jnp.concatenate(above, axis=0)
        scale = live / (TOP_PRESSURE + running)
        sigma = (TOP_PRESSURE + above + 0.5 * thick) * scale
        sig_ref[:, cols] = sigma
        share = 1.0 / (running + 1.0 - live)
        for t in range(tracers):
            mix = jnp.concatenate(
                [got[t * levels : (t + 1) * levels], got[fields + t * levels : fields + (t + 1) * levels]], axis=0
            )
            mean = jnp.sum(thick * mix, axis=0, keepdims=True) * share
            mix_ref[t * levels2 : (t + 1) * levels2, cols] = mix + MIXING_RATE * sigma * (mean - mix)


def whole(shape):
    if shape == (1,):
        return pl.BlockSpec(memory_space=pltpu.SMEM)
    return pl.BlockSpec(shape, lambda i: (0,) * len(shape))


def halved(shape, fixed=None):
    lead = (0,) * (len(shape) - 1)
    block = shape[:-1] + (shape[-1] // 2,)
    return pl.BlockSpec(block, lambda i: lead + ((i if fixed is None else fixed),))


def call(kernel, outs, ins, steps=1, ins_half=None, outs_half=(), scratch=(), vmem=40):
    ins_half = ins_half or {}
    in_specs, out_specs = [], []
    for number, value in enumerate(ins):
        if number in ins_half:
            in_specs.append(halved(value.shape, ins_half[number]))
        else:
            in_specs.append(whole(value.shape))
    for number, (shape, kind) in enumerate(outs):
        out_specs.append(halved(shape) if number in outs_half else whole(shape))
    return pl.pallas_call(
        kernel,
        grid=(steps,),
        out_shape=[jax.ShapeDtypeStruct(shape, kind) for shape, kind in outs],
        in_specs=in_specs,
        out_specs=out_specs,
        scratch_shapes=list(scratch),
        compiler_params=pltpu.CompilerParams(vmem_limit_bytes=vmem * 1024 * 1024),
    )(*ins)


def swap(value, step, parity, count, row=None):
    pairs = []
    for i in range(count - step):
        if i // step % 2 == parity and (row is None or i // row == (i + step) // row):
            pairs += [(i, i + step), (i + step, i)]
    return lax.ppermute(value, "sfc", pairs)


def body(
    tracers,
    layer_mass,
    layer_mass_next,
    wind,
    spheremp,
    inverse_mass,
    rec_peer,
    rec_slot,
    rec_flip,
    publish_list,
    column_slot_table,
):
    own_index = lax.axis_index("sfc").astype(jnp.int32)
    lev_index = lax.axis_index("lev").astype(jnp.int32)
    sfc_count = lax.axis_size("sfc")
    lev_count = lax.axis_size("lev")
    tracer_count, level_count, points, elems = tracers.shape
    fields = tracer_count * level_count
    block_cols = sfc_count // DEV_ROWS
    own = own_index.reshape(1)
    col_odd = (own_index % block_cols % 2).reshape(1)
    row_odd = (own_index // block_cols % 2).reshape(1)

    weighted, message, info = call(
        functools.partial(flux_kernel, block_cols),
        [((points, fields, elems), F32), ((fields, 256), F32), ((8, 4 * elems), jnp.int32)],
        [
            own,
            tracers.reshape(fields * points, elems),
            layer_mass.reshape(level_count * points, elems),
            wind.reshape(2 * level_count * points, elems),
            spheremp,
            rec_peer,
            rec_slot,
        ],
        steps=2,
        ins_half={1: None, 2: None, 3: None, 4: None},
        outs_half=(0,),
    )
    first = message[:, :128]
    near_a = swap(first, 1, 0, sfc_count, block_cols)
    near_b = swap(first, 1, 1, sfc_count, block_cols)
    local, far, mid = call(
        functools.partial(local_kernel, block_cols),
        [((points, fields, elems), F32), ((12, 256, elems), BF16), ((128, 128), BF16)],
        [own, weighted, rec_peer, rec_slot, rec_flip, publish_list.reshape(-1, 1), info],
    )
    got_one, second = call(
        middle_kernel,
        [((fields, 128), F32), ((fields, 128), F32)],
        [col_odd, near_a, near_b, message, mid],
    )
    over_a = swap(second, block_cols, 0, sfc_count)
    over_b = swap(second, block_cols, 1, sfc_count)
    group_width = 5 * NPG * elems // 4
    next_mass = layer_mass_next.reshape(level_count * points, elems)
    order, rden, rows = call(
        functools.partial(sort_kernel, group_width),
        [((NPG * elems, NPG * elems), BF16), ((NPG, level_count, elems), F32), ((2, sfc_count, 128), F32)],
        [column_slot_table, next_mass, next_mass, spheremp],
        ins_half={1: 0, 2: 1},
    )
    mass, send = call(
        finish_kernel,
        [((fields * points, elems), F32), ((ROWS * sfc_count, fields), F32)],
        [row_odd, local, got_one, over_a, over_b, far, spheremp, inverse_mass, rden, order, rows],
        steps=2,
        ins_half={1: None, 5: None, 6: None, 7: None, 8: None},
        outs_half=(0,),
        scratch=[pltpu.VMEM((2 * fields, NPG * elems), BF16)],
    )
    moved = lax.all_to_all(
        send.reshape(sfc_count, 1, ROWS * fields), "sfc", split_axis=0, concat_axis=0, tiled=True
    ).reshape(ROWS * sfc_count, fields)
    other = lax.ppermute(moved, "lev", [(0, 1), (1, 0)])
    slots = group_width // lev_count
    levels = level_count * lev_count
    mixed, sigma = call(
        physics_kernel,
        [((tracer_count * levels, slots), F32), ((levels, slots), F32)],
        [lev_index.reshape(1), moved, other],
    )
    return (
        mass.reshape(tracers.shape),
        mixed.reshape(tracer_count, levels, slots),
        sigma,
    )


def solution(mesh):
    in_specs = (
        P(None, "lev", None, "sfc"),
        P("lev", None, "sfc"),
        P("lev", None, "sfc"),
        P(None, "lev", None, "sfc"),
        P(None, "sfc"),
        P(None, "sfc"),
        P(None, "sfc"),
        P(None, "sfc"),
        P(None, "sfc"),
        P("sfc"),
        P(None, "sfc"),
    )
    out_specs = (
        P(None, "lev", None, "sfc"),
        P(None, None, ("sfc", "lev")),
        P(None, ("sfc", "lev")),
    )
    return jax.shard_map(body, mesh=mesh, in_specs=in_specs, out_specs=out_specs, check_vma=False)
```

```python
import functools

import jax
import jax.numpy as jnp
import numpy as np
from jax import lax
from jax.experimental import pallas as pl
from jax.experimental.pallas import tpu as pltpu
from jax.sharding import PartitionSpec as P

F32 = jnp.float32
BF16 = jnp.bfloat16
NPG = 4
DEV_ROWS = 4
SIDE_POINTS = [[0, 1, 2, 3], [3, 7, 11, 15], [12, 13, 14, 15], [0, 4, 8, 12]]
CORNER_POINTS = [0, 3, 12, 15]
CORNER_SIDES = [[(0, 0), (3, 0)], [(0, 3), (1, 0)], [(2, 0), (3, 3)], [(1, 3), (2, 3)]]
EDGE_SLOTS = [(s, m) for s in range(4) for m in (1, 2)]
POINT_NUMBER = {p: c for c, p in enumerate(CORNER_POINTS)}
POINT_NUMBER.update({SIDE_POINTS[s][m]: 4 + n for n, (s, m) in enumerate(EDGE_SLOTS)})
TIME_STEP = 0.05
TOP_PRESSURE = 1.0
MIXING_RATE = 0.8
PER_SIDE = 16
ROWS = 10


def lagrange_derivative():
    gll_points = np.array([-1.0, -1.0 / np.sqrt(5.0), 1.0 / np.sqrt(5.0), 1.0])
    barycentric = np.array(
        [
            1.0
            / np.prod(
                [gll_points[source] - gll_points[middle] for middle in range(4) if middle != source]
            )
            for source in range(4)
        ]
    )
    derivative = np.zeros((4, 4))
    for target in range(4):
        for source in range(4):
            if target != source:
                derivative[target, source] = (
                    barycentric[source]
                    / barycentric[target]
                    / (gll_points[target] - gll_points[source])
                )
        derivative[target, target] = -np.sum(derivative[target])
    return derivative


def iota(shape, dim):
    return lax.broadcasted_iota(jnp.int32, shape, dim)


def hot(mask):
    return jnp.where(mask, 1.0, 0.0).astype(BF16)


def split(x, axis=0):
    high = x.astype(BF16)
    low = (x - high.astype(F32)).astype(BF16)
    return jnp.concatenate([high, low], axis=axis)


def dot_nn(a, b):
    return lax.dot_general(a, b, (((1,), (0,)), ((), ())), preferred_element_type=F32)


def dot_nt(a, b):
    return lax.dot_general(a, b, (((1,), (1,)), ((), ())), preferred_element_type=F32)


def wide(ref, first=0):
    return jnp.concatenate([ref[first + s : first + s + 1, :] for s in range(4)], axis=1)


def facing(peer, own, block_cols):
    ahead = peer - own
    code = jnp.full_like(peer, -1)
    for number, offset in enumerate((1, -1, block_cols, -block_cols)):
        code = jnp.where(ahead == offset, number, code)
    return jnp.where(peer >= 0, code, -1)


def ranks(direction, entry):
    count = direction.shape[1]
    code = jnp.where(direction >= 0, direction * 64 + entry, -1)
    found = jnp.where(iota((256, count), 0) == code, 1.0, 0.0)
    present = jnp.max(found, axis=1, keepdims=True)
    row, col = iota((256, 256), 0), iota((256, 256), 1)
    before = hot((col < row) & (col // 64 == row // 64))
    below = dot_nn(before, jnp.broadcast_to(present, (256, 128)).astype(BF16))
    rank = jnp.sum(found * below[:, :1], axis=0, keepdims=True)
    return rank.astype(jnp.int32)


def flux_kernel(
    block_cols, own_ref, tr_hbm, lm_hbm, wd_hbm, sph_hbm, peer_hbm, slot_hbm, flip_hbm, pub_hbm, table_hbm, next_hbm, inv_hbm,
    x_ref, one_ref, two_ref, info_ref, sph_ref, peer_ref, slot_ref, flip_ref, pub_ref, table_ref, next_ref, inv_ref,
    tr_ref, lm_ref, wd_ref, sems
):
    deriv = lagrange_derivative() * TIME_STEP
    levels = lm_ref.shape[1] // 16
    tracers = tr_ref.shape[1] // lm_ref.shape[1]
    elems = peer_ref.shape[1]
    lanes = tr_ref.shape[2]
    copies = []

    def fetch(src, dst):
        copy = pltpu.make_async_copy(src, dst, sems.at[len(copies)])
        copy.start()
        copies.append(copy)
        return copy

    small = [fetch(peer_hbm, peer_ref), fetch(slot_hbm, slot_ref), fetch(sph_hbm, sph_ref)]
    big = []
    for half in range(2):
        cut = slice(half * lanes, (half + 1) * lanes)
        big.append(
            [
                fetch(lm_hbm.at[:, cut], lm_ref.at[half]),
                fetch(wd_hbm.at[:, cut], wd_ref.at[half]),
                fetch(tr_hbm.at[:, cut], tr_ref.at[half]),
            ]
        )
    later = [fetch(flip_hbm, flip_ref), fetch(pub_hbm, pub_ref), fetch(table_hbm, table_ref), fetch(inv_hbm, inv_ref)]
    for half in range(2):
        later.append(fetch(next_hbm.at[:, half * lanes : (half + 1) * lanes], next_ref.at[half]))

    for copy in small:
        copy.wait()
    direction = facing(wide(peer_ref), own_ref[0], block_cols)
    rank = ranks(direction, jnp.clip(wide(slot_ref), 0, 63))
    usable = (direction >= 0) & (rank < PER_SIDE)
    base = jnp.where(usable, direction * 64 + rank, -1000)
    info_ref[...] = jnp.broadcast_to(base, info_ref.shape)

    for half in range(2):
        cut = slice(half * lanes, (half + 1) * lanes)
        for copy in big[half]:
            copy.wait()
        tr_half, lm_half, wd_half = tr_ref.at[half], lm_ref.at[half], wd_ref.at[half]

        def one(t, carry):
            mass, fa, fb = [], [], []
            for k in range(16):
                tr = tr_half[pl.ds(t * (levels * 16) + k, levels, stride=16), :]
                mk = tr * lm_half[pl.ds(k, levels, stride=16), :]
                mass.append(mk)
                fa.append(mk * wd_half[pl.ds(k, levels, stride=16), :])
                fb.append(mk * wd_half[pl.ds(levels * 16 + k, levels, stride=16), :])
            for k in range(16):
                j, i = k // 4, k % 4
                value = mass[k]
                for other in range(4):
                    if abs(deriv[i, other]) > 1e-12:
                        value = value - deriv[i, other] * fa[4 * j + other]
                    if abs(deriv[j, other]) > 1e-12:
                        value = value - deriv[j, other] * fb[4 * other + i]
                x_ref[k, pl.ds(pl.multiple_of(t * levels, levels), levels), cut] = value * sph_ref[k : k + 1, cut]
            return carry

        lax.fori_loop(0, tracers, one, 0)

    lane = iota((256, elems), 0)
    total = None
    for group in [[pair] for pair in EDGE_SLOTS] + CORNER_SIDES:
        pick = None
        for s, m in group:
            here = lane == base[:, s * elems : (s + 1) * elems] + m * PER_SIDE
            pick = here if pick is None else pick | here
        s, m = group[0]
        part = dot_nt(split(x_ref[SIDE_POINTS[s][m]]), hot(pick))
        total = part if total is None else total + part
    fields = total.shape[0] // 2
    total = total[:fields] + total[fields:]
    one_ref[...] = total[:, :128]
    two_ref[...] = total[:, 128:]
    for copy in later:
        copy.wait()


def arrive(recv, turn, elems, s, m):
    cols = slice(s * elems, (s + 1) * elems)
    turned = jnp.where(turn[:, cols] == 1, 3 - m, m)
    return recv[:, cols] + turned * PER_SIDE


def plan_kernel(
    block_cols, group_width, own_ref, peer_ref, flip_ref, pub_ref, info_ref, table_ref, next_ref, sph_ref, held_ref,
    recv_ref, mid_ref, key_ref, rden_ref, rows_ref
):
    elems = peer_ref.shape[1]
    sides = 4 * elems
    peer, flip = wide(peer_ref), wide(flip_ref)
    at = iota((1, sides), 1)
    entries = pub_ref.shape[1]
    square = iota((entries, entries), 0) == iota((entries, entries), 1)
    listed = jnp.sum(jnp.where(square, pub_ref[...].astype(F32), 0.0), axis=1, keepdims=True).astype(jnp.int32)
    own_code = 4 * (at % elems) + at // elems
    match = jnp.where(listed == own_code, 1.0, 0.0)
    place = jnp.sum(match * iota((entries, sides), 0).astype(F32), axis=0, keepdims=True).astype(jnp.int32)
    direction = facing(peer, own_ref[0], block_cols)
    rank = ranks(direction, place)
    usable = (direction >= 0) & (rank < PER_SIDE)
    start = jnp.where(direction == 0, 64, jnp.where(direction == 1, 0, jnp.where(direction == 2, 192, 128)))
    recv = jnp.where(usable, start + rank, -1000)
    recv_ref[...] = jnp.broadcast_to(recv, recv_ref.shape)
    base = info_ref[:1, :]
    second = jnp.where(base >= 128, base - 128, -1000)
    lane = iota((128, elems), 0)
    sent, got = [], []
    for c in range(4):
        (sa, ma), (sb, mb) = CORNER_SIDES[c]
        got.append(hot((lane == arrive(recv, flip, elems, sa, ma)) | (lane == arrive(recv, flip, elems, sb, mb))))
        here = [lane == second[:, s * elems : (s + 1) * elems] + m * PER_SIDE for s, m in CORNER_SIDES[c]]
        sent.append(hot(here[0] | here[1]))
    mid_ref[...] = dot_nt(jnp.concatenate(got, axis=1), jnp.concatenate(sent, axis=1)).astype(BF16)

    levels = next_ref.shape[1] // 16
    sph = sph_ref[...]
    thicks = []
    for c in range(4):
        den, area = None, None
        for k in range(16):
            if 2 * (k // 8) + k % 4 // 2 != c:
                continue
            weight = sph[k : k + 1, :]
            term = [next_ref.at[half][pl.ds(k, levels, stride=16), :] for half in range(2)]
            term = jnp.concatenate(term, axis=1) * weight
            den = term if den is None else den + term
            area = weight if area is None else area + weight
        rden_ref[:, c * elems : (c + 1) * elems] = 1.0 / den
        thicks.append(den / area)
    thick = jnp.concatenate(thicks, axis=1)
    total = 4 * elems
    slot = wide(table_ref)
    slot_f = slot.astype(F32)
    dest = jnp.floor((slot_f + 0.5) * (1.0 / group_width)).astype(jnp.int32)
    within = (slot - dest * group_width).astype(F32)
    peers = rows_ref.shape[1]
    to = jnp.where(iota((peers, total), 0) == dest, 1.0, 0.0)
    to_b = to.astype(BF16)
    upto = hot(iota((128, 128), 0) < iota((128, 128), 1))
    before = jnp.zeros((peers, 1), F32)
    parts = []
    for block in range(total // 128):
        cols = slice(block * 128, block * 128 + 128)
        parts.append(dot_nn(to_b[:, cols], upto) + before)
        before = before + jnp.sum(to[:, cols], axis=1, keepdims=True)
    rank = jnp.sum(to * jnp.concatenate(parts, axis=1), axis=0, keepdims=True).astype(jnp.int32)
    key = dest * 8 + rank
    key_ref[...] = jnp.broadcast_to(key, key_ref.shape)
    at = iota((128, total), 0)
    spread = jnp.where(at // levels == rank, jnp.concatenate([thick] * (128 // levels), axis=0), 0.0)
    ids = jnp.where(at == rank, within, 0.0)
    both = jnp.concatenate([split(spread), split(ids)], axis=0)
    got = dot_nt(to_b, both)
    rows_ref[0] = got[:, :128] + got[:, 128:256]
    rows_ref[1] = got[:, 256:384] + got[:, 384:]


def local_kernel(
    own_ref, x_ref, peer_ref, slot_ref, flip_ref, recv_ref, sph_ref, inv_ref, rden_ref, xd_ref, far_ref, far_mix_ref, mix_ref
):
    own = own_ref[0]
    elems = peer_ref.shape[1]
    fields = x_ref.shape[1]
    sides = 4 * elems
    peer, slot, flip = wide(peer_ref), wide(slot_ref), wide(flip_ref)
    recv = recv_ref[:1, :]
    lane = iota((256, elems), 0)
    corner_far = []
    for c in range(4):
        (sa, ma), (sb, mb) = CORNER_SIDES[c]
        corner_far.append(hot((lane == arrive(recv, flip, elems, sa, ma)) | (lane == arrive(recv, flip, elems, sb, mb))))
    corner_far = jnp.concatenate(corner_far, axis=1)
    for number, (s, m) in enumerate(EDGE_SLOTS):
        far_ref[4 + number] = hot(lane == arrive(recv, flip, elems, s, m))

    local = peer == own
    slot_c = jnp.clip(slot, 0, 4 * elems - 1)
    near = jnp.where(local, slot_c % 4 * elems + slot_c // 4, -1)

    def corner_source(code, end, ok):
        side = code % 4
        corner = jnp.where(side == 1, 1, jnp.where(side == 2, 2, 0)) + end * jnp.where(side % 2 == 1, 2, 1)
        return jnp.where(ok, corner * elems + code // 4, -1)

    cpeer, cslot, cflip = wide(peer_ref, 4), wide(slot_ref, 4), wide(flip_ref, 4)
    third = corner_source(jnp.clip(cslot, 0, 4 * elems - 1), cflip, cpeer == own)
    source = iota((sides, elems), 0)
    weights = []
    for c in range(4):
        cols = slice(c * elems, (c + 1) * elems)
        weight = jnp.where(source == third[:, cols], 1.0, 0.0)
        for s, m in CORNER_SIDES[c]:
            own_cols = slice(s * elems, (s + 1) * elems)
            end = jnp.where(flip[:, own_cols] == 1, 1 - m // 3, m // 3)
            code = corner_source(slot_c[:, own_cols], end, local[:, own_cols])
            weight = weight + jnp.where(source == code, 1.0, 0.0)
        weights.append(weight.astype(BF16))
    corners = jnp.concatenate([x_ref[p] for p in CORNER_POINTS], axis=1)
    lhs = jnp.concatenate([split(corners), corner_far], axis=0)
    for c in range(4):
        cols = slice(c * elems, (c + 1) * elems)
        got = dot_nn(lhs, weights[c])
        xd_ref[CORNER_POINTS[c]] = corners[:, cols] + got[:fields] + got[fields : 2 * fields]
        far_ref[c] = corner_far[:, cols] + got[2 * fields :].astype(BF16)
    inner = []
    for m in (1, 2):
        inner.append(split(jnp.concatenate([x_ref[SIDE_POINTS[s][m]] for s in range(4)], axis=1)))
    inner = jnp.concatenate(inner, axis=0)
    for s in range(4):
        cols = slice(s * elems, (s + 1) * elems)
        got = dot_nn(inner, hot(source == near[:, cols]))
        one = got[:fields] + got[fields : 2 * fields]
        two = got[2 * fields : 3 * fields] + got[3 * fields :]
        turned = flip[:, cols] == 1
        for m, mine, swapped in ((1, one, two), (2, two, one)):
            p = SIDE_POINTS[s][m]
            xd_ref[p] = x_ref[p] + jnp.where(turned, swapped, mine)
    for p in (5, 6, 9, 10):
        xd_ref[p] = x_ref[p]

    weight = sph_ref[...] * inv_ref[...]
    levels = rden_ref.shape[0]
    for c in range(4):
        cols = slice(c * elems, (c + 1) * elems)
        mix, far_mix = None, None
        for k in range(16):
            if 2 * (k // 8) + k % 4 // 2 != c:
                continue
            wk = weight[k : k + 1, :]
            term = xd_ref[k] * wk
            mix = term if mix is None else mix + term
            if k in POINT_NUMBER:
                term = far_ref[POINT_NUMBER[k]].astype(F32) * wk
                far_mix = term if far_mix is None else far_mix + term
        mix_ref[:, cols] = mix * jnp.concatenate([rden_ref[:, cols]] * (fields // levels), axis=0)
        high = far_mix.astype(BF16)
        far_mix_ref[0, :, cols] = high
        far_mix_ref[1, :, cols] = (far_mix - high.astype(F32)).astype(BF16)


def merge(odd, a, b):
    low = iota(a.shape, 1) < 64
    lower = jnp.where(odd == 1, a, b)
    upper = jnp.where(odd == 1, b, a)
    return jnp.where(low, lower, upper)


def middle_kernel(odd_ref, a_ref, b_ref, two_ref, mid_ref, held_ref, got_ref, out_ref):
    got = merge(odd_ref[0], a_ref[...], b_ref[...])
    got_ref[...] = got
    fields = got.shape[0]
    add = dot_nn(split(got), mid_ref[...])
    out_ref[...] = two_ref[...] + add[:fields] + add[fields:]


def send_kernel(odd_ref, one_ref, a_ref, b_ref, far_mix_ref, mix_ref, rden_ref, key_ref, rows_ref, held_ref, far_held_ref, two_ref, out_ref):
    fields = mix_ref.shape[0]
    levels = rden_ref.shape[0]
    two = merge(odd_ref[0], a_ref[...], b_ref[...])
    two_ref[...] = two
    got = split(jnp.concatenate([one_ref[...], two], axis=1))
    add = dot_nn(got, far_mix_ref[0]) + dot_nn(got, far_mix_ref[1])
    add = add[:fields] + add[fields:]
    mix_hl = split(mix_ref[...] + add * jnp.concatenate([rden_ref[...]] * (fields // levels), axis=0))
    peers = rows_ref.shape[1]
    chunk = 128
    key = key_ref[:1, :]
    row_of = iota((chunk, key.shape[1]), 0)
    for block in range(peers * 8 // chunk):
        res = dot_nt(hot(row_of == key - block * chunk), mix_hl)
        res = res[:, :fields] + res[:, fields:]
        for d in range(chunk // 8):
            row = (block * (chunk // 8) + d) * ROWS
            out_ref[row : row + 8, :] = res[d * 8 : d * 8 + 8, :]
    out_ref[pl.ds(8, peers, stride=ROWS), :] = rows_ref[0]
    out_ref[pl.ds(9, peers, stride=ROWS), :] = rows_ref[1]


def mass_kernel(xd_ref, one_ref, two_ref, far_ref, inv_ref, tm_ref):
    fields = xd_ref.shape[1]
    got = split(jnp.concatenate([one_ref[...], two_ref[...]], axis=1))
    for k in range(16):
        value = xd_ref[k]
        if k in POINT_NUMBER:
            far = dot_nn(got, far_ref[POINT_NUMBER[k]])
            value = value + far[:fields] + far[fields:]
        tm_ref[pl.ds(k, fields, stride=16), :] = value * inv_ref[k : k + 1, :]


def gathered(buf_ref, pick_ref, levels):
    total, fields = buf_ref.shape
    peers = total // ROWS
    slots = pick_ref.shape[0]
    thick = buf_ref[pl.ds(8, peers, stride=ROWS), :]
    spread = hot(iota((total, peers), 0) // ROWS == iota((total, peers), 1))
    rows = dot_nn(spread, split(thick, axis=1))
    keep = iota((total, 128), 1) // levels == iota((total, 128), 0) % ROWS
    rows = split(jnp.where(keep, rows[:, :128] + rows[:, 128:], 0.0), axis=0)
    fold = hot(iota((128, 128), 1) == iota((128, 128), 0) % levels)
    narrow = dot_nn(rows, fold)
    narrow = narrow[:total] + narrow[total:]
    narrow = jnp.where(iota((total, 128), 1) == levels, 1.0, narrow)
    stack = split(jnp.concatenate([buf_ref[...], narrow], axis=1), axis=1)
    width = fields + 128
    outs = []
    for block in range(slots // 128):
        got = dot_nn(pick_ref[block * 128 : (block + 1) * 128, :], stack)
        outs.append(jnp.transpose(got[:, :width] + got[:, width:]))
    return outs


def place_kernel(lev_ref, own_ref, pick_ref, half_ref, *, levels):
    total = own_ref.shape[0]
    peers = total // ROWS
    slots = pick_ref.shape[0]
    ids = own_ref[pl.ds(9, peers, stride=ROWS), :]
    spread = hot(iota((peers, total), 1) // ROWS == iota((peers, total), 0))
    ids_t = jnp.transpose(ids)[:16, :]
    cand = dot_nn(split(ids_t), spread)
    cand = cand[:16] + cand[16:]
    spot = iota((16, total), 1) % ROWS
    key = jnp.sum(jnp.where((spot == iota((16, total), 0)) & (spot < 8), cand, 0.0), axis=0, keepdims=True)
    key = jnp.where(iota((1, total), 1) % ROWS < 8, key, -1e6).astype(jnp.int32)
    key = key - lev_ref[0] * slots
    for block in range(slots // 128):
        pick_ref[block * 128 : (block + 1) * 128, :] = hot(iota((128, total), 0) + block * 128 == key)
    for block, got in enumerate(gathered(own_ref, pick_ref, levels)):
        half_ref[:, block * 128 : (block + 1) * 128] = got


def physics_kernel(lev_ref, half_ref, par_ref, pick_ref, mix_ref, sig_ref):
    lev = lev_ref[0]
    levels2 = sig_ref.shape[0]
    fields = par_ref.shape[1]
    levels = levels2 // 2
    tracers = fields // levels
    for block, other in enumerate(gathered(par_ref, pick_ref, levels)):
        cols = slice(block * 128, (block + 1) * 128)
        mine = half_ref[:, cols]
        first = jnp.where(lev == 0, mine, other)
        last = jnp.where(lev == 0, other, mine)
        thick = jnp.concatenate([first[fields : fields + levels], last[fields : fields + levels]], axis=0)
        live = first[fields + levels : fields + levels + 1]
        running = jnp.zeros_like(live)
        above = []
        for level in range(levels2):
            above.append(running)
            running = running + thick[level : level + 1]
        above = jnp.concatenate(above, axis=0)
        scale = live / (TOP_PRESSURE + running)
        sigma = (TOP_PRESSURE + above + 0.5 * thick) * scale
        sig_ref[:, cols] = sigma
        share = 1.0 / (running + 1.0 - live)
        for t in range(tracers):
            mix = jnp.concatenate([first[t * levels : (t + 1) * levels], last[t * levels : (t + 1) * levels]], axis=0)
            mean = jnp.sum(thick * mix, axis=0, keepdims=True) * share
            mix_ref[t * levels2 : (t + 1) * levels2, cols] = mix + MIXING_RATE * sigma * (mean - mix)


def halved(shape):
    lead = (0,) * (len(shape) - 1)
    return pl.BlockSpec(shape[:-1] + (shape[-1] // 2,), lambda i: lead + (i,))


def call(kernel, outs, ins, hbm=(), held=(), scratch=(), vmem=16):
    specs = []
    for number, value in enumerate(ins):
        space = pltpu.SMEM if value.shape == (1,) else pltpu.HBM if number in hbm else pltpu.VMEM
        space = pl.ANY if number in held else space
        specs.append(pl.BlockSpec(memory_space=space))
    ins = [pltpu.with_memory_space_constraint(x, pltpu.HBM) if n in hbm else x for n, x in enumerate(ins)]
    return pl.pallas_call(
        kernel,
        out_shape=[out[2](*out[:2]) if len(out) > 2 else jax.ShapeDtypeStruct(*out) for out in outs],
        in_specs=specs,
        out_specs=[pl.BlockSpec(memory_space=out[2] if len(out) > 2 else pltpu.VMEM) for out in outs],
        scratch_shapes=list(scratch),
        compiler_params=pltpu.CompilerParams(vmem_limit_bytes=vmem * 1024 * 1024),
    )(*ins)


def swap(value, step, parity, count, row=None):
    pairs = []
    for i in range(count - step):
        if i // step % 2 == parity and (row is None or i // row == (i + step) // row):
            pairs += [(i, i + step), (i + step, i)]
    return lax.ppermute(value, "sfc", pairs)


def body(
    tracers,
    layer_mass,
    layer_mass_next,
    wind,
    spheremp,
    inverse_mass,
    rec_peer,
    rec_slot,
    rec_flip,
    publish_list,
    column_slot_table,
):
    own_index = lax.axis_index("sfc").astype(jnp.int32)
    lev_index = lax.axis_index("lev").astype(jnp.int32)
    sfc_count = lax.axis_size("sfc")
    lev_count = lax.axis_size("lev")
    tracer_count, level_count, points, elems = tracers.shape
    fields = tracer_count * level_count
    block_cols = sfc_count // DEV_ROWS
    own = own_index.reshape(1)
    col_odd = (own_index % block_cols % 2).reshape(1)
    row_odd = (own_index // block_cols % 2).reshape(1)

    rows = level_count * points
    half = elems // 2
    cols = NPG * elems
    ints = jnp.int32
    ins = [
        own,
        tracers.reshape(fields * points, elems),
        layer_mass.reshape(rows, elems),
        wind.reshape(2 * rows, elems),
        spheremp,
        rec_peer,
        rec_slot,
        rec_flip,
        publish_list.reshape(1, -1),
        column_slot_table,
        layer_mass_next.reshape(rows, elems),
        inverse_mass,
    ]
    weighted, first, second, info, sph, peer, slot, flip, pub, table, after, inv = call(
        functools.partial(flux_kernel, block_cols),
        [
            ((points, fields, elems), F32, pltpu.VMEM),
            ((fields, 128), F32),
            ((fields, 128), F32),
            ((8, 4 * elems), ints),
            (spheremp.shape, F32),
            (rec_peer.shape, ints),
            (rec_slot.shape, ints),
            (rec_flip.shape, ints),
            ((1, publish_list.shape[0]), ints),
            (column_slot_table.shape, ints),
            ((2, rows, half), F32),
            (inverse_mass.shape, F32),
        ],
        ins,
        hbm=range(1, len(ins)),
        scratch=[
            pltpu.VMEM((2, fields * points, half), F32),
            pltpu.VMEM((2, rows, half), F32),
            pltpu.VMEM((2, 2 * rows, half), F32),
            pltpu.SemaphoreType.DMA((15,)),
        ],
    )
    near_a = swap(first, 1, 0, sfc_count, block_cols)
    near_b = swap(first, 1, 1, sfc_count, block_cols)
    group_width = 5 * NPG * elems // 4
    recv, mid, key, rden, extra = call(
        functools.partial(plan_kernel, block_cols, group_width),
        [
            ((8, 4 * elems), ints),
            ((128, 128), BF16),
            ((8, cols), ints),
            ((level_count, cols), F32),
            ((2, sfc_count, 128), F32),
        ],
        [own, peer, flip, pub, info, table, after, sph, weighted],
        held=(8,),
    )
    got_one, second = call(
        middle_kernel,
        [((fields, 128), F32), ((fields, 128), F32)],
        [col_odd, near_a, near_b, second, mid, weighted],
        held=(5,),
    )
    over_a = swap(second, block_cols, 0, sfc_count)
    over_b = swap(second, block_cols, 1, sfc_count)
    weighted, _ = lax.optimization_barrier((weighted, second))
    local, far, far_mix, mix = call(
        local_kernel,
        [
            ((points, fields, elems), F32, pltpu.VMEM),
            ((12, 256, elems), BF16, pltpu.VMEM),
            ((2, 256, cols), BF16),
            ((fields, cols), F32),
        ],
        [own, weighted, peer, slot, flip, recv, sph, inv, rden],
    )
    got_two, send = call(
        send_kernel,
        [((fields, 128), F32), ((ROWS * sfc_count, fields), F32)],
        [row_odd, got_one, over_a, over_b, far_mix, mix, rden, key, extra, local, far],
        held=(9, 10),
    )
    moved = lax.all_to_all(
        send.reshape(sfc_count, 1, ROWS * fields), "sfc", split_axis=0, concat_axis=0, tiled=True
    ).reshape(ROWS * sfc_count, fields)
    whole = pl.BlockSpec((fields, 128), lambda i: (0, 0))
    mass = pl.pallas_call(
        mass_kernel,
        grid=(2,),
        out_shape=jax.ShapeDtypeStruct((fields * points, elems), F32),
        in_specs=[halved(local.shape), whole, whole, halved(far.shape), halved(inv.shape)],
        out_specs=halved((fields * points, elems)),
        compiler_params=pltpu.CompilerParams(vmem_limit_bytes=12 * 1024 * 1024),
        cost_estimate=pl.CostEstimate(flops=2 * 256 * 256 * 3072, bytes_accessed=16 * fields * points * elems, transcendentals=0),
    )(local, got_one, got_two, far, inv)
    moved, mass = lax.optimization_barrier((moved, mass))
    other = lax.ppermute(moved, "lev", [(0, 1), (1, 0)])
    slots = group_width // lev_count
    levels = level_count * lev_count
    lev = lev_index.reshape(1)
    pick, own_half = call(
        functools.partial(place_kernel, levels=level_count),
        [((slots, ROWS * sfc_count), BF16), ((fields + 128, slots), F32)],
        [lev, moved],
    )
    mixed, sigma = call(
        physics_kernel,
        [((tracer_count * levels, slots), F32), ((levels, slots), F32)],
        [lev, own_half, other, pick],
    )
    return (
        mass.reshape(tracers.shape),
        mixed.reshape(tracer_count, levels, slots),
        sigma,
    )


def solution(mesh):
    in_specs = (
        P(None, "lev", None, "sfc"),
        P("lev", None, "sfc"),
        P("lev", None, "sfc"),
        P(None, "lev", None, "sfc"),
        P(None, "sfc"),
        P(None, "sfc"),
        P(None, "sfc"),
        P(None, "sfc"),
        P(None, "sfc"),
        P("sfc"),
        P(None, "sfc"),
    )
    out_specs = (
        P(None, "lev", None, "sfc"),
        P(None, None, ("sfc", "lev")),
        P(None, ("sfc", "lev")),
    )
    return jax.shard_map(body, mesh=mesh, in_specs=in_specs, out_specs=out_specs, check_vma=False)
```

```python
import functools

import jax
import jax.numpy as jnp
import numpy as np
from jax import lax
from jax.experimental import pallas as pl
from jax.experimental.pallas import tpu as pltpu
from jax.sharding import PartitionSpec as P

F32 = jnp.float32
BF16 = jnp.bfloat16
NPG = 4
DEV_ROWS = 4
SIDE_POINTS = [[0, 1, 2, 3], [3, 7, 11, 15], [12, 13, 14, 15], [0, 4, 8, 12]]
CORNER_POINTS = [0, 3, 12, 15]
CORNER_SIDES = [[(0, 0), (3, 0)], [(0, 3), (1, 0)], [(2, 0), (3, 3)], [(1, 3), (2, 3)]]
EDGE_SLOTS = [(s, m) for s in range(4) for m in (1, 2)]
POINT_NUMBER = {p: c for c, p in enumerate(CORNER_POINTS)}
POINT_NUMBER.update({SIDE_POINTS[s][m]: 4 + n for n, (s, m) in enumerate(EDGE_SLOTS)})
TIME_STEP = 0.05
TOP_PRESSURE = 1.0
MIXING_RATE = 0.8
PER_SIDE = 16
ROWS = 10


def lagrange_derivative():
    gll_points = np.array([-1.0, -1.0 / np.sqrt(5.0), 1.0 / np.sqrt(5.0), 1.0])
    barycentric = np.array(
        [
            1.0
            / np.prod(
                [gll_points[source] - gll_points[middle] for middle in range(4) if middle != source]
            )
            for source in range(4)
        ]
    )
    derivative = np.zeros((4, 4))
    for target in range(4):
        for source in range(4):
            if target != source:
                derivative[target, source] = (
                    barycentric[source]
                    / barycentric[target]
                    / (gll_points[target] - gll_points[source])
                )
        derivative[target, target] = -np.sum(derivative[target])
    return derivative


def iota(shape, dim):
    return lax.broadcasted_iota(jnp.int32, shape, dim)


def hot(mask):
    return jnp.where(mask, 1.0, 0.0).astype(BF16)


def rows_hot(count, *codes):
    row = lax.broadcasted_iota(jnp.int16, (count, codes[0].shape[1]), 0)
    mask = None
    for code in codes:
        here = row == code.astype(jnp.int16)
        mask = here if mask is None else mask | here
    return jnp.where(mask, jnp.ones((), BF16), jnp.zeros((), BF16))


def split(x, axis=0):
    high = x.astype(BF16)
    low = (x - high.astype(F32)).astype(BF16)
    return jnp.concatenate([high, low], axis=axis)


def dot_nn(a, b):
    return lax.dot_general(a, b, (((1,), (0,)), ((), ())), preferred_element_type=F32)


def dot_nt(a, b):
    return lax.dot_general(a, b, (((1,), (1,)), ((), ())), preferred_element_type=F32)


def wide(ref, first=0):
    return jnp.concatenate([ref[first + s : first + s + 1, :] for s in range(4)], axis=1)


def facing(peer, own, block_cols):
    ahead = peer - own
    code = jnp.full_like(peer, -1)
    for number, offset in enumerate((1, -1, block_cols, -block_cols)):
        code = jnp.where(ahead == offset, number, code)
    return jnp.where(peer >= 0, code, -1)


def ranks(direction, entry):
    count = direction.shape[1]
    code = jnp.where(direction >= 0, direction * 64 + entry, -1)
    found = jnp.where(iota((256, count), 0) == code, 1.0, 0.0)
    present = jnp.max(found, axis=1, keepdims=True)
    row, col = iota((256, 256), 0), iota((256, 256), 1)
    before = hot((col < row) & (col // 64 == row // 64))
    below = dot_nn(before, jnp.broadcast_to(present, (256, 128)).astype(BF16))
    rank = jnp.sum(found * below[:, :1], axis=0, keepdims=True)
    return rank.astype(jnp.int32)


def flux_kernel(
    block_cols, own_ref, tr_hbm, lm_hbm, wd_hbm, sph_hbm, peer_hbm, slot_hbm, flip_hbm, pub_hbm, table_hbm, next_hbm, inv_hbm,
    x_ref, one_ref, two_ref, info_ref, sph_ref, peer_ref, slot_ref, flip_ref, pub_ref, table_ref, next_ref, inv_ref,
    tr_ref, lm_ref, wd_ref, flow_ref, sems
):
    deriv = lagrange_derivative() * TIME_STEP
    levels = lm_ref.shape[1] // 16
    tracers = tr_ref.shape[1] // lm_ref.shape[1]
    elems = peer_ref.shape[1]
    lanes = tr_ref.shape[2]
    copies = []

    def fetch(src, dst):
        copy = pltpu.make_async_copy(src, dst, sems.at[len(copies)])
        copy.start()
        copies.append(copy)
        return copy

    small = [fetch(peer_hbm, peer_ref), fetch(slot_hbm, slot_ref), fetch(sph_hbm, sph_ref)]
    big = []
    for half in range(2):
        cut = slice(half * lanes, (half + 1) * lanes)
        big.append(
            [
                fetch(lm_hbm.at[:, cut], lm_ref.at[half]),
                fetch(wd_hbm.at[:, cut], wd_ref.at[half]),
                fetch(tr_hbm.at[:, cut], tr_ref.at[half]),
            ]
        )
    later = [fetch(flip_hbm, flip_ref), fetch(pub_hbm, pub_ref), fetch(table_hbm, table_ref), fetch(inv_hbm, inv_ref)]
    for half in range(2):
        later.append(fetch(next_hbm.at[:, half * lanes : (half + 1) * lanes], next_ref.at[half]))

    for copy in small:
        copy.wait()
    direction = facing(wide(peer_ref), own_ref[0], block_cols)
    rank = ranks(direction, jnp.clip(wide(slot_ref), 0, 63))
    usable = (direction >= 0) & (rank < PER_SIDE)
    base = jnp.where(usable, direction * 64 + rank, -1000)
    info_ref[...] = jnp.broadcast_to(base, info_ref.shape)

    for half in range(2):
        cut = slice(half * lanes, (half + 1) * lanes)
        for copy in big[half]:
            copy.wait()
        tr_half, lm_half, wd_half = tr_ref.at[half], lm_ref.at[half], wd_ref.at[half]
        for k in range(16):
            flow_ref[0, k] = lm_half[pl.ds(k, levels, stride=16), :]
            flow_ref[1, k] = wd_half[pl.ds(k, levels, stride=16), :]
            flow_ref[2, k] = wd_half[pl.ds(levels * 16 + k, levels, stride=16), :]

        def one(t, carry):
            mass, fa, fb = [], [], []
            for k in range(16):
                tr = tr_half[pl.ds(t * (levels * 16) + k, levels, stride=16), :]
                mk = tr * flow_ref[0, k]
                mass.append(mk)
                fa.append(mk * flow_ref[1, k])
                fb.append(mk * flow_ref[2, k])
            for k in range(16):
                j, i = k // 4, k % 4
                value = mass[k]
                for other in range(4):
                    if abs(deriv[i, other]) > 1e-12:
                        value = value - deriv[i, other] * fa[4 * j + other]
                    if abs(deriv[j, other]) > 1e-12:
                        value = value - deriv[j, other] * fb[4 * other + i]
                x_ref[k, pl.ds(pl.multiple_of(t * levels, levels), levels), cut] = value * sph_ref[k : k + 1, cut]
            return carry

        lax.fori_loop(0, tracers, one, 0)

    total = None
    for group in [[pair] for pair in EDGE_SLOTS] + CORNER_SIDES:
        pick = rows_hot(256, *[base[:, s * elems : (s + 1) * elems] + m * PER_SIDE for s, m in group])
        s, m = group[0]
        part = dot_nt(split(x_ref[SIDE_POINTS[s][m]]), pick)
        total = part if total is None else total + part
    fields = total.shape[0] // 2
    total = total[:fields] + total[fields:]
    one_ref[...] = total[:, :128]
    two_ref[...] = total[:, 128:]
    for copy in later:
        copy.wait()


def arrive(recv, turn, elems, s, m):
    cols = slice(s * elems, (s + 1) * elems)
    turned = jnp.where(turn[:, cols] == 1, 3 - m, m)
    return recv[:, cols] + turned * PER_SIDE


def plan_kernel(
    block_cols, group_width, own_ref, peer_ref, flip_ref, pub_ref, info_ref, table_ref, next_ref, sph_ref, held_ref,
    recv_ref, mid_ref, key_ref, rden_ref, rows_ref
):
    elems = peer_ref.shape[1]
    sides = 4 * elems
    peer, flip = wide(peer_ref), wide(flip_ref)
    at = iota((1, sides), 1)
    entries = pub_ref.shape[1]
    square = iota((entries, entries), 0) == iota((entries, entries), 1)
    listed = jnp.sum(jnp.where(square, pub_ref[...].astype(F32), 0.0), axis=1, keepdims=True).astype(jnp.int32)
    own_code = 4 * (at % elems) + at // elems
    match = jnp.where(listed == own_code, 1.0, 0.0)
    place = jnp.sum(match * iota((entries, sides), 0).astype(F32), axis=0, keepdims=True).astype(jnp.int32)
    direction = facing(peer, own_ref[0], block_cols)
    rank = ranks(direction, place)
    usable = (direction >= 0) & (rank < PER_SIDE)
    start = jnp.where(direction == 0, 64, jnp.where(direction == 1, 0, jnp.where(direction == 2, 192, 128)))
    recv = jnp.where(usable, start + rank, -1000)
    recv_ref[...] = jnp.broadcast_to(recv, recv_ref.shape)
    base = info_ref[:1, :]
    second = jnp.where(base >= 128, base - 128, -1000)
    sent, got = [], []
    for c in range(4):
        got.append(rows_hot(128, *[arrive(recv, flip, elems, s, m) for s, m in CORNER_SIDES[c]]))
        sent.append(rows_hot(128, *[second[:, s * elems : (s + 1) * elems] + m * PER_SIDE for s, m in CORNER_SIDES[c]]))
    mid_ref[...] = dot_nt(jnp.concatenate(got, axis=1), jnp.concatenate(sent, axis=1)).astype(BF16)

    levels = next_ref.shape[1] // 16
    sph = sph_ref[...]
    thicks = []
    for c in range(4):
        den, area = None, None
        for k in range(16):
            if 2 * (k // 8) + k % 4 // 2 != c:
                continue
            weight = sph[k : k + 1, :]
            term = [next_ref.at[half][pl.ds(k, levels, stride=16), :] for half in range(2)]
            term = jnp.concatenate(term, axis=1) * weight
            den = term if den is None else den + term
            area = weight if area is None else area + weight
        rden_ref[:, c * elems : (c + 1) * elems] = 1.0 / den
        thicks.append(den / area)
    thick = jnp.concatenate(thicks, axis=1)
    total = 4 * elems
    slot = wide(table_ref)
    slot_f = slot.astype(F32)
    dest = jnp.floor((slot_f + 0.5) * (1.0 / group_width)).astype(jnp.int32)
    within = (slot - dest * group_width).astype(F32)
    peers = rows_ref.shape[1]
    to = jnp.where(iota((peers, total), 0) == dest, 1.0, 0.0)
    to_b = to.astype(BF16)
    upto = hot(iota((128, 128), 0) < iota((128, 128), 1))
    before = jnp.zeros((peers, 1), F32)
    parts = []
    for block in range(total // 128):
        cols = slice(block * 128, block * 128 + 128)
        parts.append(dot_nn(to_b[:, cols], upto) + before)
        before = before + jnp.sum(to[:, cols], axis=1, keepdims=True)
    rank = jnp.sum(to * jnp.concatenate(parts, axis=1), axis=0, keepdims=True).astype(jnp.int32)
    key = dest * 8 + rank
    key_ref[...] = jnp.broadcast_to(key, key_ref.shape)
    at = iota((128, total), 0)
    spread = jnp.where(at // levels == rank, jnp.concatenate([thick] * (128 // levels), axis=0), 0.0)
    ids = jnp.where(at == rank, within, 0.0)
    both = jnp.concatenate([split(spread), split(ids)], axis=0)
    got = dot_nt(to_b, both)
    rows_ref[0] = got[:, :128] + got[:, 128:256]
    rows_ref[1] = got[:, 256:384] + got[:, 384:]


def local_kernel(
    own_ref, x_ref, peer_ref, slot_ref, flip_ref, recv_ref, sph_ref, inv_ref, rden_ref, xd_ref, far_ref, far_mix_ref, mix_ref
):
    own = own_ref[0]
    elems = peer_ref.shape[1]
    fields = x_ref.shape[1]
    sides = 4 * elems
    peer, slot, flip = wide(peer_ref), wide(slot_ref), wide(flip_ref)
    recv = recv_ref[:1, :]
    corner_far = []
    for c in range(4):
        corner_far.append(rows_hot(256, *[arrive(recv, flip, elems, s, m) for s, m in CORNER_SIDES[c]]))
    corner_far = jnp.concatenate(corner_far, axis=1)
    for number, (s, m) in enumerate(EDGE_SLOTS):
        far_ref[4 + number] = rows_hot(256, arrive(recv, flip, elems, s, m))

    local = peer == own
    slot_c = jnp.clip(slot, 0, 4 * elems - 1)
    near = jnp.where(local, slot_c % 4 * elems + slot_c // 4, -1)

    def corner_source(code, end, ok):
        side = code % 4
        corner = jnp.where(side == 1, 1, jnp.where(side == 2, 2, 0)) + end * jnp.where(side % 2 == 1, 2, 1)
        return jnp.where(ok, corner * elems + code // 4, -1)

    cpeer, cslot, cflip = wide(peer_ref, 4), wide(slot_ref, 4), wide(flip_ref, 4)
    third = corner_source(jnp.clip(cslot, 0, 4 * elems - 1), cflip, cpeer == own)
    weights = []
    for c in range(4):
        cols = slice(c * elems, (c + 1) * elems)
        codes = [third[:, cols]]
        for s, m in CORNER_SIDES[c]:
            own_cols = slice(s * elems, (s + 1) * elems)
            end = jnp.where(flip[:, own_cols] == 1, 1 - m // 3, m // 3)
            codes.append(corner_source(slot_c[:, own_cols], end, local[:, own_cols]))
        weights.append(rows_hot(sides, *codes))
    corners = jnp.concatenate([x_ref[p] for p in CORNER_POINTS], axis=1)
    lhs = jnp.concatenate([split(corners), corner_far], axis=0)
    for c in range(4):
        cols = slice(c * elems, (c + 1) * elems)
        got = dot_nn(lhs, weights[c])
        xd_ref[CORNER_POINTS[c]] = corners[:, cols] + got[:fields] + got[fields : 2 * fields]
        far_ref[c] = corner_far[:, cols] + got[2 * fields :].astype(BF16)
    inner = []
    for m in (1, 2):
        inner.append(split(jnp.concatenate([x_ref[SIDE_POINTS[s][m]] for s in range(4)], axis=1)))
    inner = jnp.concatenate(inner, axis=0)
    for s in range(4):
        cols = slice(s * elems, (s + 1) * elems)
        got = dot_nn(inner, rows_hot(sides, near[:, cols]))
        one = got[:fields] + got[fields : 2 * fields]
        two = got[2 * fields : 3 * fields] + got[3 * fields :]
        turned = flip[:, cols] == 1
        for m, mine, swapped in ((1, one, two), (2, two, one)):
            p = SIDE_POINTS[s][m]
            xd_ref[p] = x_ref[p] + jnp.where(turned, swapped, mine)
    for p in (5, 6, 9, 10):
        xd_ref[p] = x_ref[p]

    weight = sph_ref[...] * inv_ref[...]
    levels = rden_ref.shape[0]
    for c in range(4):
        cols = slice(c * elems, (c + 1) * elems)
        mix, far_mix = None, None
        for k in range(16):
            if 2 * (k // 8) + k % 4 // 2 != c:
                continue
            wk = weight[k : k + 1, :]
            term = xd_ref[k] * wk
            mix = term if mix is None else mix + term
            if k in POINT_NUMBER:
                term = far_ref[POINT_NUMBER[k]].astype(F32) * wk
                far_mix = term if far_mix is None else far_mix + term
        mix_ref[:, cols] = mix * jnp.concatenate([rden_ref[:, cols]] * (fields // levels), axis=0)
        high = far_mix.astype(BF16)
        far_mix_ref[0, :, cols] = high
        far_mix_ref[1, :, cols] = (far_mix - high.astype(F32)).astype(BF16)


def merge(odd, a, b):
    low = iota(a.shape, 1) < 64
    lower = jnp.where(odd == 1, a, b)
    upper = jnp.where(odd == 1, b, a)
    return jnp.where(low, lower, upper)


def middle_kernel(odd_ref, a_ref, b_ref, two_ref, mid_ref, held_ref, got_ref, out_ref):
    got = merge(odd_ref[0], a_ref[...], b_ref[...])
    got_ref[...] = got
    fields = got.shape[0]
    add = dot_nn(split(got), mid_ref[...])
    out_ref[...] = two_ref[...] + add[:fields] + add[fields:]


def send_kernel(odd_ref, one_ref, a_ref, b_ref, far_mix_ref, mix_ref, rden_ref, key_ref, rows_ref, held_ref, far_held_ref, two_ref, out_ref):
    fields = mix_ref.shape[0]
    levels = rden_ref.shape[0]
    two = merge(odd_ref[0], a_ref[...], b_ref[...])
    two_ref[...] = two
    got = split(jnp.concatenate([one_ref[...], two], axis=1))
    add = dot_nn(got, far_mix_ref[0]) + dot_nn(got, far_mix_ref[1])
    add = add[:fields] + add[fields:]
    mix_hl = split(mix_ref[...] + add * jnp.concatenate([rden_ref[...]] * (fields // levels), axis=0))
    peers = rows_ref.shape[1]
    chunk = 512
    key = key_ref[:1, :]
    for block in range(peers * 8 // chunk):
        res = dot_nt(rows_hot(chunk, key - block * chunk), mix_hl)
        res = res[:, :fields] + res[:, fields:]
        for d in range(chunk // 8):
            row = (block * (chunk // 8) + d) * ROWS
            out_ref[row : row + 8, :] = res[d * 8 : d * 8 + 8, :]
    out_ref[pl.ds(8, peers, stride=ROWS), :] = rows_ref[0]
    out_ref[pl.ds(9, peers, stride=ROWS), :] = rows_ref[1]


def mass_kernel(xd_ref, one_ref, two_ref, far_ref, inv_ref, tm_ref, frame_ref):
    @pl.when(pl.program_id(0) == 0)
    def _():
        total = frame_ref.shape[0]
        row, lane = iota((total, 128), 0), iota((total, 128), 1)
        source = row // ROWS
        frame_ref[:, :128] = hot(lane == source)
        frame_ref[:, 128:] = hot(lane // 16 == row - ROWS * source)

    fields = xd_ref.shape[1]
    got = split(jnp.concatenate([one_ref[...], two_ref[...]], axis=1))
    for k in range(16):
        value = xd_ref[k]
        if k in POINT_NUMBER:
            far = dot_nn(got, far_ref[POINT_NUMBER[k]])
            value = value + far[:fields] + far[fields:]
        tm_ref[pl.ds(k, fields, stride=16), :] = value * inv_ref[k : k + 1, :]


def gathered(buf_ref, pick_ref, meta_ref, levels):
    total = buf_ref.shape[0]
    peers = total // ROWS
    slots = pick_ref.shape[0]
    meta = meta_ref[...]
    thick = dot_nn(meta[:, :128], split(buf_ref[pl.ds(8, peers, stride=ROWS), :], axis=1))
    thick = (thick[:, :128] + thick[:, 128:]) * meta[:, 128:].astype(F32)
    row, lane = iota((384, 128), 0), iota((384, 128), 1)
    fold = hot(jnp.where(row < 256, row % levels, levels) == lane)
    narrow = dot_nn(jnp.concatenate([split(thick, axis=1), meta[:, :128]], axis=1), fold)
    stack = split(buf_ref[...], axis=1)
    outs = []
    for block in range(slots // 128):
        rows = slice(block * 128, (block + 1) * 128)
        got = dot_nn(pick_ref[rows, :], stack)
        outs.append(jnp.concatenate([jnp.transpose(got[:, :128] + got[:, 128:]), jnp.transpose(narrow[rows])], axis=0))
    return outs


def place_kernel(lev_ref, own_ref, frame_ref, pick_ref, meta_ref, half_ref, *, levels):
    total = own_ref.shape[0]
    peers = total // ROWS
    slots = pick_ref.shape[0]
    ids = own_ref[pl.ds(9, peers, stride=ROWS), :]
    ids_t = jnp.transpose(ids)[:16, :]
    cand = dot_nt(split(ids_t), frame_ref[:, :128])
    cand = cand[:16] + cand[16:]
    spot = iota((16, total), 1) % ROWS
    key = jnp.sum(jnp.where((spot == iota((16, total), 0)) & (spot < 8), cand, 0.0), axis=0, keepdims=True)
    key = jnp.where(iota((1, total), 1) % ROWS < 8, key, -9999.0).astype(jnp.int32)
    key = key - lev_ref[0] * slots
    for block in range(slots // 128):
        rows = slice(block * 128, (block + 1) * 128)
        pick_ref[rows, :] = rows_hot(128, key - block * 128)
        meta_ref[rows, :] = dot_nn(pick_ref[rows, :], frame_ref[...]).astype(BF16)
    for block, got in enumerate(gathered(own_ref, pick_ref, meta_ref, levels)):
        half_ref[:, block * 128 : (block + 1) * 128] = got


def physics_kernel(lev_ref, half_ref, par_ref, pick_ref, meta_ref, mix_ref, sig_ref):
    lev = lev_ref[0]
    levels2 = sig_ref.shape[0]
    fields = par_ref.shape[1]
    levels = levels2 // 2
    tracers = fields // levels
    for block, other in enumerate(gathered(par_ref, pick_ref, meta_ref, levels)):
        cols = slice(block * 128, (block + 1) * 128)
        mine = half_ref[:, cols]
        first = jnp.where(lev == 0, mine, other)
        last = jnp.where(lev == 0, other, mine)
        thick = jnp.concatenate([first[fields : fields + levels], last[fields : fields + levels]], axis=0)
        live = first[fields + levels : fields + levels + 1]
        running = jnp.zeros_like(live)
        above = []
        for level in range(levels2):
            above.append(running)
            running = running + thick[level : level + 1]
        above = jnp.concatenate(above, axis=0)
        scale = live / (TOP_PRESSURE + running)
        sigma = (TOP_PRESSURE + above + 0.5 * thick) * scale
        sig_ref[:, cols] = sigma
        share = 1.0 / (running + 1.0 - live)
        for t in range(tracers):
            mix = jnp.concatenate([first[t * levels : (t + 1) * levels], last[t * levels : (t + 1) * levels]], axis=0)
            mean = jnp.sum(thick * mix, axis=0, keepdims=True) * share
            mix_ref[t * levels2 : (t + 1) * levels2, cols] = mix + MIXING_RATE * sigma * (mean - mix)


def halved(shape):
    lead = (0,) * (len(shape) - 1)
    return pl.BlockSpec(shape[:-1] + (shape[-1] // 2,), lambda i: lead + (i,))


def call(kernel, outs, ins, hbm=(), held=(), scratch=(), vmem=16):
    specs = []
    for number, value in enumerate(ins):
        space = pltpu.SMEM if value.shape == (1,) else pltpu.HBM if number in hbm else pltpu.VMEM
        space = pl.ANY if number in held else space
        specs.append(pl.BlockSpec(memory_space=space))
    ins = [pltpu.with_memory_space_constraint(x, pltpu.HBM) if n in hbm else x for n, x in enumerate(ins)]
    return pl.pallas_call(
        kernel,
        out_shape=[out[2](*out[:2]) if len(out) > 2 else jax.ShapeDtypeStruct(*out) for out in outs],
        in_specs=specs,
        out_specs=[pl.BlockSpec(memory_space=out[2] if len(out) > 2 else pltpu.VMEM) for out in outs],
        scratch_shapes=list(scratch),
        compiler_params=pltpu.CompilerParams(vmem_limit_bytes=vmem * 1024 * 1024),
    )(*ins)


def swap(value, step, parity, count, row=None):
    pairs = []
    for i in range(count - step):
        if i // step % 2 == parity and (row is None or i // row == (i + step) // row):
            pairs += [(i, i + step), (i + step, i)]
    return lax.ppermute(value, "sfc", pairs)


def body(
    tracers,
    layer_mass,
    layer_mass_next,
    wind,
    spheremp,
    inverse_mass,
    rec_peer,
    rec_slot,
    rec_flip,
    publish_list,
    column_slot_table,
):
    own_index = lax.axis_index("sfc").astype(jnp.int32)
    lev_index = lax.axis_index("lev").astype(jnp.int32)
    sfc_count = lax.axis_size("sfc")
    lev_count = lax.axis_size("lev")
    tracer_count, level_count, points, elems = tracers.shape
    fields = tracer_count * level_count
    block_cols = sfc_count // DEV_ROWS
    own = own_index.reshape(1)
    col_odd = (own_index % block_cols % 2).reshape(1)
    row_odd = (own_index // block_cols % 2).reshape(1)

    rows = level_count * points
    half = elems // 2
    cols = NPG * elems
    ints = jnp.int32
    ins = [
        own,
        tracers.reshape(fields * points, elems),
        layer_mass.reshape(rows, elems),
        wind.reshape(2 * rows, elems),
        spheremp,
        rec_peer,
        rec_slot,
        rec_flip,
        publish_list.reshape(1, -1),
        column_slot_table,
        layer_mass_next.reshape(rows, elems),
        inverse_mass,
    ]
    weighted, first, second, info, sph, peer, slot, flip, pub, table, after, inv = call(
        functools.partial(flux_kernel, block_cols),
        [
            ((points, fields, elems), F32, pltpu.VMEM),
            ((fields, 128), F32),
            ((fields, 128), F32),
            ((8, 4 * elems), ints),
            (spheremp.shape, F32),
            (rec_peer.shape, ints),
            (rec_slot.shape, ints),
            (rec_flip.shape, ints),
            ((1, publish_list.shape[0]), ints),
            (column_slot_table.shape, ints),
            ((2, rows, half), F32),
            (inverse_mass.shape, F32),
        ],
        ins,
        hbm=range(1, len(ins)),
        scratch=[
            pltpu.VMEM((2, fields * points, half), F32),
            pltpu.VMEM((2, rows, half), F32),
            pltpu.VMEM((2, 2 * rows, half), F32),
            pltpu.VMEM((3, points, level_count, half), F32),
            pltpu.SemaphoreType.DMA((15,)),
        ],
    )
    near_a = swap(first, 1, 0, sfc_count, block_cols)
    near_b = swap(first, 1, 1, sfc_count, block_cols)
    group_width = 5 * NPG * elems // 4
    recv, mid, key, rden, extra = call(
        functools.partial(plan_kernel, block_cols, group_width),
        [
            ((8, 4 * elems), ints),
            ((128, 128), BF16),
            ((8, cols), ints),
            ((level_count, cols), F32),
            ((2, sfc_count, 128), F32),
        ],
        [own, peer, flip, pub, info, table, after, sph, weighted],
        held=(8,),
    )
    got_one, second = call(
        middle_kernel,
        [((fields, 128), F32), ((fields, 128), F32)],
        [col_odd, near_a, near_b, second, mid, weighted],
        held=(5,),
    )
    over_a = swap(second, block_cols, 0, sfc_count)
    over_b = swap(second, block_cols, 1, sfc_count)
    weighted, _ = lax.optimization_barrier((weighted, second))
    local, far, far_mix, mix = call(
        local_kernel,
        [
            ((points, fields, elems), F32, pltpu.VMEM),
            ((12, 256, elems), BF16, pltpu.VMEM),
            ((2, 256, cols), BF16),
            ((fields, cols), F32),
        ],
        [own, weighted, peer, slot, flip, recv, sph, inv, rden],
    )
    got_two, send = call(
        send_kernel,
        [((fields, 128), F32), ((ROWS * sfc_count, fields), F32)],
        [row_odd, got_one, over_a, over_b, far_mix, mix, rden, key, extra, local, far],
        held=(9, 10),
    )
    moved = lax.all_to_all(
        send.reshape(sfc_count, 1, ROWS * fields), "sfc", split_axis=0, concat_axis=0, tiled=True
    ).reshape(ROWS * sfc_count, fields)
    whole = pl.BlockSpec((fields, 128), lambda i: (0, 0))
    mass, frame = pl.pallas_call(
        mass_kernel,
        grid=(2,),
        out_shape=[
            jax.ShapeDtypeStruct((fields * points, elems), F32),
            jax.ShapeDtypeStruct((ROWS * sfc_count, 256), BF16),
        ],
        in_specs=[halved(local.shape), whole, whole, halved(far.shape), halved(inv.shape)],
        out_specs=[halved((fields * points, elems)), pl.BlockSpec((ROWS * sfc_count, 256), lambda i: (0, 0))],
        compiler_params=pltpu.CompilerParams(vmem_limit_bytes=12 * 1024 * 1024),
        cost_estimate=pl.CostEstimate(flops=2 * 256 * 256 * 3072, bytes_accessed=16 * fields * points * elems, transcendentals=0),
    )(local, got_one, got_two, far, inv)
    moved, mass, frame = lax.optimization_barrier((moved, mass, frame))
    other = lax.ppermute(moved, "lev", [(0, 1), (1, 0)])
    slots = group_width // lev_count
    levels = level_count * lev_count
    lev = lev_index.reshape(1)
    pick, meta, own_half = call(
        functools.partial(place_kernel, levels=level_count),
        [((slots, ROWS * sfc_count), BF16), ((slots, 256), BF16), ((fields + 128, slots), F32)],
        [lev, moved, frame],
    )
    mixed, sigma = call(
        physics_kernel,
        [((tracer_count * levels, slots), F32), ((levels, slots), F32)],
        [lev, own_half, other, pick, meta],
    )
    return (
        mass.reshape(tracers.shape),
        mixed.reshape(tracer_count, levels, slots),
        sigma,
    )


def solution(mesh):
    in_specs = (
        P(None, "lev", None, "sfc"),
        P("lev", None, "sfc"),
        P("lev", None, "sfc"),
        P(None, "lev", None, "sfc"),
        P(None, "sfc"),
        P(None, "sfc"),
        P(None, "sfc"),
        P(None, "sfc"),
        P(None, "sfc"),
        P("sfc"),
        P(None, "sfc"),
    )
    out_specs = (
        P(None, "lev", None, "sfc"),
        P(None, None, ("sfc", "lev")),
        P(None, ("sfc", "lev")),
    )
    return jax.shard_map(body, mesh=mesh, in_specs=in_specs, out_specs=out_specs, check_vma=False)
```

```python
import functools

import jax
import jax.numpy as jnp
import numpy as np
from jax import lax
from jax.experimental import pallas as pl
from jax.experimental.pallas import tpu as pltpu
from jax.sharding import PartitionSpec as P

F32 = jnp.float32
BF16 = jnp.bfloat16
NPG = 4
DEV_ROWS = 4
SIDE_POINTS = [[0, 1, 2, 3], [3, 7, 11, 15], [12, 13, 14, 15], [0, 4, 8, 12]]
CORNER_POINTS = [0, 3, 12, 15]
CORNER_SIDES = [[(0, 0), (3, 0)], [(0, 3), (1, 0)], [(2, 0), (3, 3)], [(1, 3), (2, 3)]]
EDGE_SLOTS = [(s, m) for s in range(4) for m in (1, 2)]
POINT_NUMBER = {p: c for c, p in enumerate(CORNER_POINTS)}
POINT_NUMBER.update({SIDE_POINTS[s][m]: 4 + n for n, (s, m) in enumerate(EDGE_SLOTS)})
TIME_STEP = 0.05
TOP_PRESSURE = 1.0
MIXING_RATE = 0.8
PER_SIDE = 16
ROWS = 10


def lagrange_derivative():
    gll_points = np.array([-1.0, -1.0 / np.sqrt(5.0), 1.0 / np.sqrt(5.0), 1.0])
    barycentric = np.array(
        [
            1.0
            / np.prod(
                [gll_points[source] - gll_points[middle] for middle in range(4) if middle != source]
            )
            for source in range(4)
        ]
    )
    derivative = np.zeros((4, 4))
    for target in range(4):
        for source in range(4):
            if target != source:
                derivative[target, source] = (
                    barycentric[source]
                    / barycentric[target]
                    / (gll_points[target] - gll_points[source])
                )
        derivative[target, target] = -np.sum(derivative[target])
    return derivative


def iota(shape, dim):
    return lax.broadcasted_iota(jnp.int32, shape, dim)


def hot(mask):
    return jnp.where(mask, 1.0, 0.0).astype(BF16)


def rows_hot(count, *codes):
    row = lax.broadcasted_iota(jnp.int16, (count, codes[0].shape[1]), 0)
    mask = None
    for code in codes:
        here = row == code.astype(jnp.int16)
        mask = here if mask is None else mask | here
    return jnp.where(mask, jnp.ones((), BF16), jnp.zeros((), BF16))


def split(x, axis=0):
    high = x.astype(BF16)
    low = (x - high.astype(F32)).astype(BF16)
    return jnp.concatenate([high, low], axis=axis)


def dot_nn(a, b):
    return lax.dot_general(a, b, (((1,), (0,)), ((), ())), preferred_element_type=F32)


def dot_nt(a, b):
    return lax.dot_general(a, b, (((1,), (1,)), ((), ())), preferred_element_type=F32)


def wide(ref, first=0):
    return jnp.concatenate([ref[first + s : first + s + 1, :] for s in range(4)], axis=1)


def facing(peer, own, block_cols):
    ahead = peer - own
    code = jnp.full_like(peer, -1)
    for number, offset in enumerate((1, -1, block_cols, -block_cols)):
        code = jnp.where(ahead == offset, number, code)
    return jnp.where(peer >= 0, code, -1)


def ranks(direction, entry):
    count = direction.shape[1]
    code = jnp.where(direction >= 0, direction * 64 + entry, -1)
    found = jnp.where(iota((256, count), 0) == code, 1.0, 0.0)
    present = jnp.max(found, axis=1, keepdims=True)
    row, col = iota((256, 256), 0), iota((256, 256), 1)
    before = hot((col < row) & (col // 64 == row // 64))
    below = dot_nn(before, jnp.broadcast_to(present, (256, 128)).astype(BF16))
    rank = jnp.sum(found * below[:, :1], axis=0, keepdims=True)
    return rank.astype(jnp.int32)


def flux_kernel(
    block_cols, own_ref, odd_ref, tr_hbm, lm_hbm, wd_hbm, sph_hbm, peer_hbm, slot_hbm, flip_hbm, pub_hbm, table_hbm, next_hbm, inv_hbm,
    x_ref, one_a_ref, one_b_ref, two_ref, info_ref, sph_ref, peer_ref, slot_ref, flip_ref, pub_ref, table_ref, next_ref, inv_ref,
    tr_ref, lm_ref, wd_ref, flow_ref, sems
):
    deriv = lagrange_derivative() * TIME_STEP
    levels = lm_ref.shape[1] // 16
    tracers = tr_ref.shape[1] // lm_ref.shape[1]
    elems = peer_ref.shape[1]
    lanes = tr_ref.shape[2]
    copies = []

    def fetch(src, dst):
        copy = pltpu.make_async_copy(src, dst, sems.at[len(copies)])
        copy.start()
        copies.append(copy)
        return copy

    small = [fetch(peer_hbm, peer_ref), fetch(slot_hbm, slot_ref), fetch(sph_hbm, sph_ref)]
    big = []
    for half in range(2):
        cut = slice(half * lanes, (half + 1) * lanes)
        big.append(
            [
                fetch(lm_hbm.at[:, cut], lm_ref.at[half]),
                fetch(wd_hbm.at[:, cut], wd_ref.at[half]),
                fetch(tr_hbm.at[:, cut], tr_ref.at[half]),
            ]
        )
    for copy in small:
        copy.wait()
    direction = facing(wide(peer_ref), own_ref[0], block_cols)
    rank = ranks(direction, jnp.clip(wide(slot_ref), 0, 63))
    usable = (direction >= 0) & (rank < PER_SIDE)
    base = jnp.where(usable, direction * 64 + rank, -1000)
    info_ref[...] = jnp.broadcast_to(base, info_ref.shape)
    later = [fetch(flip_hbm, flip_ref), fetch(pub_hbm, pub_ref), fetch(table_hbm, table_ref), fetch(inv_hbm, inv_ref)]
    for half in range(2):
        later.append(fetch(next_hbm.at[:, half * lanes : (half + 1) * lanes], next_ref.at[half]))

    for half in range(2):
        cut = slice(half * lanes, (half + 1) * lanes)
        for copy in big[half]:
            copy.wait()
        tr_half, lm_half, wd_half = tr_ref.at[half], lm_ref.at[half], wd_ref.at[half]
        for k in range(16):
            flow_ref[0, k] = lm_half[pl.ds(k, levels, stride=16), :]
            flow_ref[1, k] = wd_half[pl.ds(k, levels, stride=16), :]
            flow_ref[2, k] = wd_half[pl.ds(levels * 16 + k, levels, stride=16), :]

        def one(t, carry):
            mass, fa, fb = [], [], []
            for k in range(16):
                tr = tr_half[pl.ds(t * (levels * 16) + k, levels, stride=16), :]
                mk = tr * flow_ref[0, k]
                mass.append(mk)
                fa.append(mk * flow_ref[1, k])
                fb.append(mk * flow_ref[2, k])
            for k in range(16):
                j, i = k // 4, k % 4
                value = mass[k]
                for other in range(4):
                    if abs(deriv[i, other]) > 1e-12:
                        value = value - deriv[i, other] * fa[4 * j + other]
                    if abs(deriv[j, other]) > 1e-12:
                        value = value - deriv[j, other] * fb[4 * other + i]
                x_ref[k, pl.ds(pl.multiple_of(t * levels, levels), levels), cut] = value * sph_ref[k : k + 1, cut]
            return carry

        lax.fori_loop(0, tracers, one, 0)

    total = None
    for group in [[pair] for pair in EDGE_SLOTS] + CORNER_SIDES:
        pick = rows_hot(256, *[base[:, s * elems : (s + 1) * elems] + m * PER_SIDE for s, m in group])
        s, m = group[0]
        part = dot_nt(split(x_ref[SIDE_POINTS[s][m]]), pick)
        total = part if total is None else total + part
    fields = total.shape[0] // 2
    total = total[:fields] + total[fields:]
    one_a_ref[...], one_b_ref[...] = pack(odd_ref[0], total[:, :128])
    two_ref[...] = total[:, 128:]
    for copy in later:
        copy.wait()


def arrive(recv, turn, elems, s, m):
    cols = slice(s * elems, (s + 1) * elems)
    turned = jnp.where(turn[:, cols] == 1, 3 - m, m)
    return recv[:, cols] + turned * PER_SIDE


def plan_kernel(
    block_cols, group_width, own_ref, peer_ref, flip_ref, pub_ref, info_ref, table_ref, next_ref, sph_ref, held_ref,
    recv_ref, mid_ref, key_ref, rden_ref, rows_ref
):
    elems = peer_ref.shape[1]
    sides = 4 * elems
    peer, flip = wide(peer_ref), wide(flip_ref)
    at = iota((1, sides), 1)
    entries = pub_ref.shape[1]
    square = iota((entries, entries), 0) == iota((entries, entries), 1)
    listed = jnp.sum(jnp.where(square, pub_ref[...].astype(F32), 0.0), axis=1, keepdims=True).astype(jnp.int32)
    own_code = 4 * (at % elems) + at // elems
    match = jnp.where(listed == own_code, 1.0, 0.0)
    place = jnp.sum(match * iota((entries, sides), 0).astype(F32), axis=0, keepdims=True).astype(jnp.int32)
    direction = facing(peer, own_ref[0], block_cols)
    rank = ranks(direction, place)
    usable = (direction >= 0) & (rank < PER_SIDE)
    start = jnp.where(direction == 0, 64, jnp.where(direction == 1, 0, jnp.where(direction == 2, 192, 128)))
    recv = jnp.where(usable, start + rank, -1000)
    recv_ref[...] = jnp.broadcast_to(recv, recv_ref.shape)
    base = info_ref[:1, :]
    second = jnp.where(base >= 128, base - 128, -1000)
    sent, got = [], []
    for c in range(4):
        got.append(rows_hot(128, *[arrive(recv, flip, elems, s, m) for s, m in CORNER_SIDES[c]]))
        sent.append(rows_hot(128, *[second[:, s * elems : (s + 1) * elems] + m * PER_SIDE for s, m in CORNER_SIDES[c]]))
    mid_ref[...] = dot_nt(jnp.concatenate(got, axis=1), jnp.concatenate(sent, axis=1)).astype(BF16)

    levels = next_ref.shape[1] // 16
    sph = sph_ref[...]
    thicks = []
    for c in range(4):
        den, area = None, None
        for k in range(16):
            if 2 * (k // 8) + k % 4 // 2 != c:
                continue
            weight = sph[k : k + 1, :]
            term = [next_ref.at[half][pl.ds(k, levels, stride=16), :] for half in range(2)]
            term = jnp.concatenate(term, axis=1) * weight
            den = term if den is None else den + term
            area = weight if area is None else area + weight
        rden_ref[:, c * elems : (c + 1) * elems] = 1.0 / den
        thicks.append(den / area)
    thick = jnp.concatenate(thicks, axis=1)
    total = 4 * elems
    slot = wide(table_ref)
    slot_f = slot.astype(F32)
    dest = jnp.floor((slot_f + 0.5) * (1.0 / group_width)).astype(jnp.int32)
    within = (slot - dest * group_width).astype(F32)
    peers = rows_ref.shape[1]
    to = jnp.where(iota((peers, total), 0) == dest, 1.0, 0.0)
    to_b = to.astype(BF16)
    upto = hot(iota((128, 128), 0) < iota((128, 128), 1))
    before = jnp.zeros((peers, 1), F32)
    parts = []
    for block in range(total // 128):
        cols = slice(block * 128, block * 128 + 128)
        parts.append(dot_nn(to_b[:, cols], upto) + before)
        before = before + jnp.sum(to[:, cols], axis=1, keepdims=True)
    rank = jnp.sum(to * jnp.concatenate(parts, axis=1), axis=0, keepdims=True).astype(jnp.int32)
    key = dest * 8 + rank
    key_ref[...] = jnp.broadcast_to(key, key_ref.shape)
    at = iota((128, total), 0)
    spread = jnp.where(at // levels == rank, jnp.concatenate([thick] * (128 // levels), axis=0), 0.0)
    ids = jnp.where(at == rank, within, 0.0)
    both = jnp.concatenate([split(spread), split(ids)], axis=0)
    got = dot_nt(to_b, both)
    rows_ref[0] = got[:, :128] + got[:, 128:256]
    rows_ref[1] = got[:, 256:384] + got[:, 384:]


def local_kernel(
    own_ref, x_ref, peer_ref, slot_ref, flip_ref, recv_ref, sph_ref, inv_ref, rden_ref, xd_ref, far_ref, far_mix_ref, mix_ref
):
    own = own_ref[0]
    elems = peer_ref.shape[1]
    fields = x_ref.shape[1]
    sides = 4 * elems
    peer, slot, flip = wide(peer_ref), wide(slot_ref), wide(flip_ref)
    recv = recv_ref[:1, :]
    corner_far = []
    for c in range(4):
        corner_far.append(rows_hot(256, *[arrive(recv, flip, elems, s, m) for s, m in CORNER_SIDES[c]]))
    corner_far = jnp.concatenate(corner_far, axis=1)
    for number, (s, m) in enumerate(EDGE_SLOTS):
        far_ref[4 + number] = rows_hot(256, arrive(recv, flip, elems, s, m))

    local = peer == own
    slot_c = jnp.clip(slot, 0, 4 * elems - 1)
    near = jnp.where(local, slot_c % 4 * elems + slot_c // 4, -1)

    def corner_source(code, end, ok):
        side = code % 4
        corner = jnp.where(side == 1, 1, jnp.where(side == 2, 2, 0)) + end * jnp.where(side % 2 == 1, 2, 1)
        return jnp.where(ok, corner * elems + code // 4, -1)

    cpeer, cslot, cflip = wide(peer_ref, 4), wide(slot_ref, 4), wide(flip_ref, 4)
    third = corner_source(jnp.clip(cslot, 0, 4 * elems - 1), cflip, cpeer == own)
    weights = []
    for c in range(4):
        cols = slice(c * elems, (c + 1) * elems)
        codes = [third[:, cols]]
        for s, m in CORNER_SIDES[c]:
            own_cols = slice(s * elems, (s + 1) * elems)
            end = jnp.where(flip[:, own_cols] == 1, 1 - m // 3, m // 3)
            codes.append(corner_source(slot_c[:, own_cols], end, local[:, own_cols]))
        weights.append(rows_hot(sides, *codes))
    corners = jnp.concatenate([x_ref[p] for p in CORNER_POINTS], axis=1)
    lhs = jnp.concatenate([split(corners), corner_far], axis=0)
    for c in range(4):
        cols = slice(c * elems, (c + 1) * elems)
        got = dot_nn(lhs, weights[c])
        xd_ref[CORNER_POINTS[c]] = corners[:, cols] + got[:fields] + got[fields : 2 * fields]
        far_ref[c] = corner_far[:, cols] + got[2 * fields :].astype(BF16)
    inner = []
    for m in (1, 2):
        inner.append(split(jnp.concatenate([x_ref[SIDE_POINTS[s][m]] for s in range(4)], axis=1)))
    inner = jnp.concatenate(inner, axis=0)
    for s in range(4):
        cols = slice(s * elems, (s + 1) * elems)
        got = dot_nn(inner, rows_hot(sides, near[:, cols]))
        one = got[:fields] + got[fields : 2 * fields]
        two = got[2 * fields : 3 * fields] + got[3 * fields :]
        turned = flip[:, cols] == 1
        for m, mine, swapped in ((1, one, two), (2, two, one)):
            p = SIDE_POINTS[s][m]
            xd_ref[p] = x_ref[p] + jnp.where(turned, swapped, mine)
    for p in (5, 6, 9, 10):
        xd_ref[p] = x_ref[p]

    weight = sph_ref[...] * inv_ref[...]
    levels = rden_ref.shape[0]
    for c in range(4):
        cols = slice(c * elems, (c + 1) * elems)
        mix, far_mix = None, None
        for k in range(16):
            if 2 * (k // 8) + k % 4 // 2 != c:
                continue
            wk = weight[k : k + 1, :]
            term = xd_ref[k] * wk
            mix = term if mix is None else mix + term
            if k in POINT_NUMBER:
                term = far_ref[POINT_NUMBER[k]].astype(F32) * wk
                far_mix = term if far_mix is None else far_mix + term
        mix_ref[:, cols] = mix * jnp.concatenate([rden_ref[:, cols]] * (fields // levels), axis=0)
        high = far_mix.astype(BF16)
        far_mix_ref[0, :, cols] = high
        far_mix_ref[1, :, cols] = (far_mix - high.astype(F32)).astype(BF16)


def pack(odd, msg):
    half = msg.shape[0] // 2
    low = iota((half, 128), 1) < 64
    top, bottom = msg[:half], msg[half:]
    above = jnp.where(low, top, pltpu.roll(bottom, 64, 1))
    below = jnp.where(low, pltpu.roll(top, 64, 1), bottom)
    return jnp.where(odd == 1, below, above), jnp.where(odd == 1, above, below)


def merge(odd, a, b):
    low = iota(a.shape, 1) < 64
    lower = jnp.where(odd == 1, a, b)
    upper = jnp.where(odd == 1, b, a)
    top = jnp.where(low, lower, pltpu.roll(upper, 64, 1))
    bottom = jnp.where(low, pltpu.roll(lower, 64, 1), upper)
    return jnp.concatenate([top, bottom], axis=0)


def middle_kernel(odd_ref, row_odd_ref, a_ref, b_ref, two_ref, mid_ref, held_ref, got_ref, out_a_ref, out_b_ref):
    got = merge(odd_ref[0], a_ref[...], b_ref[...])
    got_ref[...] = got
    fields = got.shape[0]
    add = dot_nn(split(got), mid_ref[...])
    msg = two_ref[...] + add[:fields] + add[fields:]
    out_a_ref[...], out_b_ref[...] = pack(row_odd_ref[0], msg)


def send_kernel(odd_ref, one_ref, a_ref, b_ref, far_mix_ref, mix_ref, rden_ref, key_ref, rows_ref, held_ref, far_held_ref, two_ref, out_ref):
    fields = mix_ref.shape[0]
    levels = rden_ref.shape[0]
    two = merge(odd_ref[0], a_ref[...], b_ref[...])
    two_ref[...] = two
    got = split(jnp.concatenate([one_ref[...], two], axis=1))
    add = dot_nn(got, far_mix_ref[0]) + dot_nn(got, far_mix_ref[1])
    add = add[:fields] + add[fields:]
    mix_hl = split(mix_ref[...] + add * jnp.concatenate([rden_ref[...]] * (fields // levels), axis=0))
    peers = rows_ref.shape[1]
    chunk = 512
    key = key_ref[:1, :]
    for block in range(peers * 8 // chunk):
        res = dot_nt(rows_hot(chunk, key - block * chunk), mix_hl)
        res = res[:, :fields] + res[:, fields:]
        for d in range(chunk // 8):
            row = (block * (chunk // 8) + d) * ROWS
            out_ref[row : row + 8, :] = res[d * 8 : d * 8 + 8, :]
    out_ref[pl.ds(8, peers, stride=ROWS), :] = rows_ref[0]
    out_ref[pl.ds(9, peers, stride=ROWS), :] = rows_ref[1]


def mass_kernel(xd_ref, one_ref, two_ref, far_ref, inv_ref, tm_ref, frame_ref):
    @pl.when(pl.program_id(0) == 0)
    def _():
        total = frame_ref.shape[0]
        row, lane = iota((total, 128), 0), iota((total, 128), 1)
        source = row // ROWS
        frame_ref[:, :128] = hot(lane == source)
        frame_ref[:, 128:] = hot(lane // 16 == row - ROWS * source)

    fields = xd_ref.shape[1]
    got = split(jnp.concatenate([one_ref[...], two_ref[...]], axis=1))
    for k in range(16):
        value = xd_ref[k]
        if k in POINT_NUMBER:
            far = dot_nn(got, far_ref[POINT_NUMBER[k]])
            value = value + far[:fields] + far[fields:]
        tm_ref[pl.ds(k, fields, stride=16), :] = value * inv_ref[k : k + 1, :]


def gathered(buf_ref, pick_ref, meta_ref, levels):
    total = buf_ref.shape[0]
    peers = total // ROWS
    slots = pick_ref.shape[0]
    meta = meta_ref[...]
    thick = dot_nn(meta[:, :128], split(buf_ref[pl.ds(8, peers, stride=ROWS), :], axis=1))
    thick = (thick[:, :128] + thick[:, 128:]) * meta[:, 128:].astype(F32)
    row, lane = iota((384, 128), 0), iota((384, 128), 1)
    fold = hot(jnp.where(row < 256, row % levels, levels) == lane)
    narrow = dot_nn(jnp.concatenate([split(thick, axis=1), meta[:, :128]], axis=1), fold)
    stack = split(buf_ref[...], axis=1)
    outs = []
    for block in range(slots // 128):
        rows = slice(block * 128, (block + 1) * 128)
        got = dot_nn(pick_ref[rows, :], stack)
        outs.append(jnp.concatenate([jnp.transpose(got[:, :128] + got[:, 128:]), jnp.transpose(narrow[rows])], axis=0))
    return outs


def place_kernel(lev_ref, own_ref, frame_ref, pick_ref, meta_ref, half_ref, *, levels):
    total = own_ref.shape[0]
    peers = total // ROWS
    slots = pick_ref.shape[0]
    ids = own_ref[pl.ds(9, peers, stride=ROWS), :]
    ids_t = jnp.transpose(ids)[:16, :]
    cand = dot_nt(split(ids_t), frame_ref[:, :128])
    cand = cand[:16] + cand[16:]
    spot = iota((16, total), 1) % ROWS
    key = jnp.sum(jnp.where((spot == iota((16, total), 0)) & (spot < 8), cand, 0.0), axis=0, keepdims=True)
    key = jnp.where(iota((1, total), 1) % ROWS < 8, key, -9999.0).astype(jnp.int32)
    key = key - lev_ref[0] * slots
    for block in range(slots // 128):
        rows = slice(block * 128, (block + 1) * 128)
        pick_ref[rows, :] = rows_hot(128, key - block * 128)
        meta_ref[rows, :] = dot_nn(pick_ref[rows, :], frame_ref[...]).astype(BF16)
    for block, got in enumerate(gathered(own_ref, pick_ref, meta_ref, levels)):
        half_ref[:, block * 128 : (block + 1) * 128] = got


def physics_kernel(lev_ref, half_ref, par_ref, pick_ref, meta_ref, mix_ref, sig_ref):
    lev = lev_ref[0]
    levels2 = sig_ref.shape[0]
    fields = par_ref.shape[1]
    levels = levels2 // 2
    tracers = fields // levels
    for block, other in enumerate(gathered(par_ref, pick_ref, meta_ref, levels)):
        cols = slice(block * 128, (block + 1) * 128)
        mine = half_ref[:, cols]
        first = jnp.where(lev == 0, mine, other)
        last = jnp.where(lev == 0, other, mine)
        thick = jnp.concatenate([first[fields : fields + levels], last[fields : fields + levels]], axis=0)
        live = first[fields + levels : fields + levels + 1]
        running = jnp.zeros_like(live)
        above = []
        for level in range(levels2):
            above.append(running)
            running = running + thick[level : level + 1]
        above = jnp.concatenate(above, axis=0)
        scale = live / (TOP_PRESSURE + running)
        sigma = (TOP_PRESSURE + above + 0.5 * thick) * scale
        sig_ref[:, cols] = sigma
        share = 1.0 / (running + 1.0 - live)
        for t in range(tracers):
            mix = jnp.concatenate([first[t * levels : (t + 1) * levels], last[t * levels : (t + 1) * levels]], axis=0)
            mean = jnp.sum(thick * mix, axis=0, keepdims=True) * share
            mix_ref[t * levels2 : (t + 1) * levels2, cols] = mix + MIXING_RATE * sigma * (mean - mix)


def halved(shape):
    lead = (0,) * (len(shape) - 1)
    return pl.BlockSpec(shape[:-1] + (shape[-1] // 2,), lambda i: lead + (i,))


def call(kernel, outs, ins, hbm=(), held=(), scratch=(), vmem=16):
    specs = []
    for number, value in enumerate(ins):
        space = pltpu.SMEM if value.shape == (1,) else pltpu.HBM if number in hbm else pltpu.VMEM
        space = pl.ANY if number in held else space
        specs.append(pl.BlockSpec(memory_space=space))
    ins = [pltpu.with_memory_space_constraint(x, pltpu.HBM) if n in hbm else x for n, x in enumerate(ins)]
    return pl.pallas_call(
        kernel,
        out_shape=[out[2](*out[:2]) if len(out) > 2 else jax.ShapeDtypeStruct(*out) for out in outs],
        in_specs=specs,
        out_specs=[pl.BlockSpec(memory_space=out[2] if len(out) > 2 else pltpu.VMEM) for out in outs],
        scratch_shapes=list(scratch),
        compiler_params=pltpu.CompilerParams(vmem_limit_bytes=vmem * 1024 * 1024),
    )(*ins)


def swap(value, step, parity, count, row=None):
    pairs = []
    for i in range(count - step):
        if i // step % 2 == parity and (row is None or i // row == (i + step) // row):
            pairs += [(i, i + step), (i + step, i)]
    return lax.ppermute(value, "sfc", pairs)


def body(
    tracers,
    layer_mass,
    layer_mass_next,
    wind,
    spheremp,
    inverse_mass,
    rec_peer,
    rec_slot,
    rec_flip,
    publish_list,
    column_slot_table,
):
    own_index = lax.axis_index("sfc").astype(jnp.int32)
    lev_index = lax.axis_index("lev").astype(jnp.int32)
    sfc_count = lax.axis_size("sfc")
    lev_count = lax.axis_size("lev")
    tracer_count, level_count, points, elems = tracers.shape
    fields = tracer_count * level_count
    block_cols = sfc_count // DEV_ROWS
    own = own_index.reshape(1)
    col_odd = (own_index % block_cols % 2).reshape(1)
    row_odd = (own_index // block_cols % 2).reshape(1)

    rows = level_count * points
    half = elems // 2
    cols = NPG * elems
    ints = jnp.int32
    ins = [
        own,
        col_odd,
        tracers.reshape(fields * points, elems),
        layer_mass.reshape(rows, elems),
        wind.reshape(2 * rows, elems),
        spheremp,
        rec_peer,
        rec_slot,
        rec_flip,
        publish_list.reshape(1, -1),
        column_slot_table,
        layer_mass_next.reshape(rows, elems),
        inverse_mass,
    ]
    weighted, first_a, first_b, second, info, sph, peer, slot, flip, pub, table, after, inv = call(
        functools.partial(flux_kernel, block_cols),
        [
            ((points, fields, elems), F32, pltpu.VMEM),
            ((fields // 2, 128), F32),
            ((fields // 2, 128), F32),
            ((fields, 128), F32),
            ((8, 4 * elems), ints),
            (spheremp.shape, F32),
            (rec_peer.shape, ints),
            (rec_slot.shape, ints),
            (rec_flip.shape, ints),
            ((1, publish_list.shape[0]), ints),
            (column_slot_table.shape, ints),
            ((2, rows, half), F32),
            (inverse_mass.shape, F32),
        ],
        ins,
        hbm=range(2, len(ins)),
        scratch=[
            pltpu.VMEM((2, fields * points, half), F32),
            pltpu.VMEM((2, rows, half), F32),
            pltpu.VMEM((2, 2 * rows, half), F32),
            pltpu.VMEM((3, points, level_count, half), F32),
            pltpu.SemaphoreType.DMA((15,)),
        ],
    )
    near_a = swap(first_a, 1, 0, sfc_count, block_cols)
    near_b = swap(first_b, 1, 1, sfc_count, block_cols)
    group_width = 5 * NPG * elems // 4
    recv, mid, key, rden, extra = call(
        functools.partial(plan_kernel, block_cols, group_width),
        [
            ((8, 4 * elems), ints),
            ((128, 128), BF16),
            ((8, cols), ints),
            ((level_count, cols), F32),
            ((2, sfc_count, 128), F32),
        ],
        [own, peer, flip, pub, info, table, after, sph, weighted],
        held=(8,),
    )
    got_one, second_a, second_b = call(
        middle_kernel,
        [((fields, 128), F32), ((fields // 2, 128), F32), ((fields // 2, 128), F32)],
        [col_odd, row_odd, near_a, near_b, second, mid, weighted],
        held=(6,),
    )
    over_a = swap(second_a, block_cols, 0, sfc_count)
    over_b = swap(second_b, block_cols, 1, sfc_count)
    weighted, _ = lax.optimization_barrier((weighted, second_a))
    local, far, far_mix, mix = call(
        local_kernel,
        [
            ((points, fields, elems), F32, pltpu.VMEM),
            ((12, 256, elems), BF16, pltpu.VMEM),
            ((2, 256, cols), BF16),
            ((fields, cols), F32),
        ],
        [own, weighted, peer, slot, flip, recv, sph, inv, rden],
    )
    got_two, send = call(
        send_kernel,
        [((fields, 128), F32), ((ROWS * sfc_count, fields), F32)],
        [row_odd, got_one, over_a, over_b, far_mix, mix, rden, key, extra, local, far],
        held=(9, 10),
    )
    moved = lax.all_to_all(
        send.reshape(sfc_count, 1, ROWS * fields), "sfc", split_axis=0, concat_axis=0, tiled=True
    ).reshape(ROWS * sfc_count, fields)
    whole = pl.BlockSpec((fields, 128), lambda i: (0, 0))
    mass, frame = pl.pallas_call(
        mass_kernel,
        grid=(2,),
        out_shape=[
            jax.ShapeDtypeStruct((fields * points, elems), F32),
            jax.ShapeDtypeStruct((ROWS * sfc_count, 256), BF16),
        ],
        in_specs=[halved(local.shape), whole, whole, halved(far.shape), halved(inv.shape)],
        out_specs=[halved((fields * points, elems)), pl.BlockSpec((ROWS * sfc_count, 256), lambda i: (0, 0))],
        compiler_params=pltpu.CompilerParams(vmem_limit_bytes=12 * 1024 * 1024),
        cost_estimate=pl.CostEstimate(flops=2 * 256 * 256 * 3072, bytes_accessed=16 * fields * points * elems, transcendentals=0),
    )(local, got_one, got_two, far, inv)
    moved, mass, frame = lax.optimization_barrier((moved, mass, frame))
    other = lax.ppermute(moved, "lev", [(0, 1), (1, 0)])
    slots = group_width // lev_count
    levels = level_count * lev_count
    lev = lev_index.reshape(1)
    pick, meta, own_half = call(
        functools.partial(place_kernel, levels=level_count),
        [((slots, ROWS * sfc_count), BF16), ((slots, 256), BF16), ((fields + 128, slots), F32)],
        [lev, moved, frame],
    )
    mixed, sigma = call(
        physics_kernel,
        [((tracer_count * levels, slots), F32), ((levels, slots), F32)],
        [lev, own_half, other, pick, meta],
    )
    return (
        mass.reshape(tracers.shape),
        mixed.reshape(tracer_count, levels, slots),
        sigma,
    )


def solution(mesh):
    in_specs = (
        P(None, "lev", None, "sfc"),
        P("lev", None, "sfc"),
        P("lev", None, "sfc"),
        P(None, "lev", None, "sfc"),
        P(None, "sfc"),
        P(None, "sfc"),
        P(None, "sfc"),
        P(None, "sfc"),
        P(None, "sfc"),
        P("sfc"),
        P(None, "sfc"),
    )
    out_specs = (
        P(None, "lev", None, "sfc"),
        P(None, None, ("sfc", "lev")),
        P(None, ("sfc", "lev")),
    )
    return jax.shard_map(body, mesh=mesh, in_specs=in_specs, out_specs=out_specs, check_vma=False)
```

```python
import functools

import jax
import jax.numpy as jnp
import numpy as np
from jax import lax
from jax.experimental import pallas as pl
from jax.experimental.pallas import tpu as pltpu
from jax.sharding import PartitionSpec as P

F32 = jnp.float32
BF16 = jnp.bfloat16
NPG = 4
DEV_ROWS = 4
SIDE_POINTS = [[0, 1, 2, 3], [3, 7, 11, 15], [12, 13, 14, 15], [0, 4, 8, 12]]
CORNER_POINTS = [0, 3, 12, 15]
CORNER_SIDES = [[(0, 0), (3, 0)], [(0, 3), (1, 0)], [(2, 0), (3, 3)], [(1, 3), (2, 3)]]
EDGE_SLOTS = [(s, m) for s in range(4) for m in (1, 2)]
POINT_NUMBER = {p: c for c, p in enumerate(CORNER_POINTS)}
POINT_NUMBER.update({SIDE_POINTS[s][m]: 4 + n for n, (s, m) in enumerate(EDGE_SLOTS)})
TIME_STEP = 0.05
TOP_PRESSURE = 1.0
MIXING_RATE = 0.8
PER_SIDE = 16
ROWS = 10


def lagrange_derivative():
    gll_points = np.array([-1.0, -1.0 / np.sqrt(5.0), 1.0 / np.sqrt(5.0), 1.0])
    barycentric = np.array(
        [
            1.0
            / np.prod(
                [gll_points[source] - gll_points[middle] for middle in range(4) if middle != source]
            )
            for source in range(4)
        ]
    )
    derivative = np.zeros((4, 4))
    for target in range(4):
        for source in range(4):
            if target != source:
                derivative[target, source] = (
                    barycentric[source]
                    / barycentric[target]
                    / (gll_points[target] - gll_points[source])
                )
        derivative[target, target] = -np.sum(derivative[target])
    return derivative


def iota(shape, dim):
    return lax.broadcasted_iota(jnp.int32, shape, dim)


def hot(mask):
    return jnp.where(mask, 1.0, 0.0).astype(BF16)


def rows_hot(count, *codes):
    row = lax.broadcasted_iota(jnp.int16, (count, codes[0].shape[1]), 0)
    mask = None
    for code in codes:
        here = row == code.astype(jnp.int16)
        mask = here if mask is None else mask | here
    return jnp.where(mask, jnp.ones((), BF16), jnp.zeros((), BF16))


def split(x, axis=0):
    high = x.astype(BF16)
    low = (x - high.astype(F32)).astype(BF16)
    return jnp.concatenate([high, low], axis=axis)


def dot_nn(a, b):
    return lax.dot_general(a, b, (((1,), (0,)), ((), ())), preferred_element_type=F32)


def dot_nt(a, b):
    return lax.dot_general(a, b, (((1,), (1,)), ((), ())), preferred_element_type=F32)


def wide(ref, first=0):
    return jnp.concatenate([ref[first + s : first + s + 1, :] for s in range(4)], axis=1)


def facing(peer, own, block_cols):
    ahead = peer - own
    code = jnp.full_like(peer, -1)
    for number, offset in enumerate((1, -1, block_cols, -block_cols)):
        code = jnp.where(ahead == offset, number, code)
    return jnp.where(peer >= 0, code, -1)


def ranks(direction, entry):
    count = direction.shape[1]
    code = jnp.where(direction >= 0, direction * 64 + entry, -1)
    found = jnp.where(iota((256, count), 0) == code, 1.0, 0.0)
    present = jnp.max(found, axis=1, keepdims=True)
    row, col = iota((256, 256), 0), iota((256, 256), 1)
    before = hot((col < row) & (col // 64 == row // 64))
    below = dot_nn(before, jnp.broadcast_to(present, (256, 128)).astype(BF16))
    rank = jnp.sum(found * below[:, :1], axis=0, keepdims=True)
    return rank.astype(jnp.int32)


def flux_kernel(
    block_cols, own_ref, odd_ref, tr_hbm, lm_hbm, wd_hbm, sph_hbm, peer_hbm, slot_hbm, flip_hbm, pub_hbm, table_hbm, next_hbm, inv_hbm,
    x_ref, one_a_ref, one_b_ref, two_ref, info_ref, sph_ref, peer_ref, slot_ref, flip_ref, pub_ref, table_ref, next_ref, inv_ref,
    tr_ref, lm_ref, wd_ref, flow_ref, sems
):
    deriv = lagrange_derivative() * TIME_STEP
    levels = lm_ref.shape[1] // 16
    tracers = tr_ref.shape[1] // lm_ref.shape[1]
    elems = peer_ref.shape[1]
    lanes = tr_ref.shape[2]
    copies = []

    def fetch(src, dst):
        copy = pltpu.make_async_copy(src, dst, sems.at[len(copies)])
        copy.start()
        copies.append(copy)
        return copy

    small = [fetch(peer_hbm, peer_ref), fetch(slot_hbm, slot_ref), fetch(sph_hbm, sph_ref)]
    big = []
    for half in range(2):
        cut = slice(half * lanes, (half + 1) * lanes)
        big.append(
            [
                fetch(lm_hbm.at[:, cut], lm_ref.at[half]),
                fetch(wd_hbm.at[:, cut], wd_ref.at[half]),
            ]
        )
        for part in range(2):
            rows = pl.ds(part * (tr_ref.shape[1] // 2), tr_ref.shape[1] // 2)
            big[half].append(fetch(tr_hbm.at[rows, cut], tr_ref.at[half, rows]))
    for copy in small:
        copy.wait()
    direction = facing(wide(peer_ref), own_ref[0], block_cols)
    rank = ranks(direction, jnp.clip(wide(slot_ref), 0, 63))
    usable = (direction >= 0) & (rank < PER_SIDE)
    base = jnp.where(usable, direction * 64 + rank, -1000)
    info_ref[...] = jnp.broadcast_to(base, info_ref.shape)
    later = [fetch(flip_hbm, flip_ref), fetch(pub_hbm, pub_ref), fetch(table_hbm, table_ref), fetch(inv_hbm, inv_ref)]
    for half in range(2):
        later.append(fetch(next_hbm.at[:, half * lanes : (half + 1) * lanes], next_ref.at[half]))

    for half in range(2):
        cut = slice(half * lanes, (half + 1) * lanes)
        for copy in big[half][:2]:
            copy.wait()
        tr_half, lm_half, wd_half = tr_ref.at[half], lm_ref.at[half], wd_ref.at[half]
        for k in range(16):
            flow_ref[0, k] = lm_half[pl.ds(k, levels, stride=16), :]
            flow_ref[1, k] = wd_half[pl.ds(k, levels, stride=16), :]
            flow_ref[2, k] = wd_half[pl.ds(levels * 16 + k, levels, stride=16), :]

        def one(t, carry):
            mass, fa, fb = [], [], []
            for k in range(16):
                tr = tr_half[pl.ds(t * (levels * 16) + k, levels, stride=16), :]
                mk = tr * flow_ref[0, k]
                mass.append(mk)
                fa.append(mk * flow_ref[1, k])
                fb.append(mk * flow_ref[2, k])
            for k in range(16):
                j, i = k // 4, k % 4
                value = mass[k]
                for other in range(4):
                    if abs(deriv[i, other]) > 1e-12:
                        value = value - deriv[i, other] * fa[4 * j + other]
                    if abs(deriv[j, other]) > 1e-12:
                        value = value - deriv[j, other] * fb[4 * other + i]
                x_ref[k, pl.ds(pl.multiple_of(t * levels, levels), levels), cut] = value * sph_ref[k : k + 1, cut]
            return carry

        for part in range(2):
            big[half][2 + part].wait()
            lax.fori_loop(part * (tracers // 2), (part + 1) * (tracers // 2), one, 0)

    total = None
    for group in [[pair] for pair in EDGE_SLOTS] + CORNER_SIDES:
        pick = rows_hot(256, *[base[:, s * elems : (s + 1) * elems] + m * PER_SIDE for s, m in group])
        s, m = group[0]
        part = dot_nt(split(x_ref[SIDE_POINTS[s][m]]), pick)
        total = part if total is None else total + part
    fields = total.shape[0] // 2
    total = total[:fields] + total[fields:]
    one_a_ref[...], one_b_ref[...] = pack(odd_ref[0], total[:, :128])
    two_ref[...] = total[:, 128:]
    for copy in later:
        copy.wait()


def arrive(recv, turn, elems, s, m):
    cols = slice(s * elems, (s + 1) * elems)
    turned = jnp.where(turn[:, cols] == 1, 3 - m, m)
    return recv[:, cols] + turned * PER_SIDE


def plan_kernel(
    block_cols, group_width, own_ref, peer_ref, flip_ref, pub_ref, info_ref, table_ref, next_ref, sph_ref, held_ref,
    recv_ref, mid_ref, key_ref, rden_ref, rows_ref
):
    elems = peer_ref.shape[1]
    sides = 4 * elems
    peer, flip = wide(peer_ref), wide(flip_ref)
    at = iota((1, sides), 1)
    entries = pub_ref.shape[1]
    square = iota((entries, entries), 0) == iota((entries, entries), 1)
    listed = jnp.sum(jnp.where(square, pub_ref[...].astype(F32), 0.0), axis=1, keepdims=True).astype(jnp.int32)
    own_code = 4 * (at % elems) + at // elems
    match = jnp.where(listed == own_code, 1.0, 0.0)
    place = jnp.sum(match * iota((entries, sides), 0).astype(F32), axis=0, keepdims=True).astype(jnp.int32)
    direction = facing(peer, own_ref[0], block_cols)
    rank = ranks(direction, place)
    usable = (direction >= 0) & (rank < PER_SIDE)
    start = jnp.where(direction == 0, 64, jnp.where(direction == 1, 0, jnp.where(direction == 2, 192, 128)))
    recv = jnp.where(usable, start + rank, -1000)
    recv_ref[...] = jnp.broadcast_to(recv, recv_ref.shape)
    base = info_ref[:1, :]
    second = jnp.where(base >= 128, base - 128, -1000)
    sent, got = [], []
    for c in range(4):
        got.append(rows_hot(128, *[arrive(recv, flip, elems, s, m) for s, m in CORNER_SIDES[c]]))
        sent.append(rows_hot(128, *[second[:, s * elems : (s + 1) * elems] + m * PER_SIDE for s, m in CORNER_SIDES[c]]))
    mid_ref[...] = dot_nt(jnp.concatenate(got, axis=1), jnp.concatenate(sent, axis=1)).astype(BF16)

    levels = next_ref.shape[1] // 16
    sph = sph_ref[...]
    thicks = []
    for c in range(4):
        den, area = None, None
        for k in range(16):
            if 2 * (k // 8) + k % 4 // 2 != c:
                continue
            weight = sph[k : k + 1, :]
            term = [next_ref.at[half][pl.ds(k, levels, stride=16), :] for half in range(2)]
            term = jnp.concatenate(term, axis=1) * weight
            den = term if den is None else den + term
            area = weight if area is None else area + weight
        rden_ref[:, c * elems : (c + 1) * elems] = 1.0 / den
        thicks.append(den / area)
    thick = jnp.concatenate(thicks, axis=1)
    total = 4 * elems
    slot = wide(table_ref)
    slot_f = slot.astype(F32)
    dest = jnp.floor((slot_f + 0.5) * (1.0 / group_width)).astype(jnp.int32)
    within = (slot - dest * group_width).astype(F32)
    peers = rows_ref.shape[1]
    to = jnp.where(iota((peers, total), 0) == dest, 1.0, 0.0)
    to_b = to.astype(BF16)
    upto = hot(iota((128, 128), 0) < iota((128, 128), 1))
    before = jnp.zeros((peers, 1), F32)
    parts = []
    for block in range(total // 128):
        cols = slice(block * 128, block * 128 + 128)
        parts.append(dot_nn(to_b[:, cols], upto) + before)
        before = before + jnp.sum(to[:, cols], axis=1, keepdims=True)
    rank = jnp.sum(to * jnp.concatenate(parts, axis=1), axis=0, keepdims=True).astype(jnp.int32)
    key = dest * 8 + rank
    key_ref[...] = jnp.broadcast_to(key, key_ref.shape)
    at = iota((128, total), 0)
    spread = jnp.where(at // levels == rank, jnp.concatenate([thick] * (128 // levels), axis=0), 0.0)
    ids = jnp.where(at == rank, within, 0.0)
    both = jnp.concatenate([split(spread), split(ids)], axis=0)
    got = dot_nt(to_b, both)
    rows_ref[0] = got[:, :128] + got[:, 128:256]
    rows_ref[1] = got[:, 256:384] + got[:, 384:]


def local_kernel(
    own_ref, x_ref, peer_ref, slot_ref, flip_ref, recv_ref, sph_ref, inv_ref, rden_ref, xd_ref, far_ref, far_mix_ref, mix_ref
):
    own = own_ref[0]
    elems = peer_ref.shape[1]
    fields = x_ref.shape[1]
    sides = 4 * elems
    peer, slot, flip = wide(peer_ref), wide(slot_ref), wide(flip_ref)
    recv = recv_ref[:1, :]
    corner_far = []
    for c in range(4):
        corner_far.append(rows_hot(256, *[arrive(recv, flip, elems, s, m) for s, m in CORNER_SIDES[c]]))
    corner_far = jnp.concatenate(corner_far, axis=1)
    for number, (s, m) in enumerate(EDGE_SLOTS):
        far_ref[4 + number] = rows_hot(256, arrive(recv, flip, elems, s, m))

    local = peer == own
    slot_c = jnp.clip(slot, 0, 4 * elems - 1)
    near = jnp.where(local, slot_c % 4 * elems + slot_c // 4, -1)

    def corner_source(code, end, ok):
        side = code % 4
        corner = jnp.where(side == 1, 1, jnp.where(side == 2, 2, 0)) + end * jnp.where(side % 2 == 1, 2, 1)
        return jnp.where(ok, corner * elems + code // 4, -1)

    cpeer, cslot, cflip = wide(peer_ref, 4), wide(slot_ref, 4), wide(flip_ref, 4)
    third = corner_source(jnp.clip(cslot, 0, 4 * elems - 1), cflip, cpeer == own)
    weights = []
    for c in range(4):
        cols = slice(c * elems, (c + 1) * elems)
        codes = [third[:, cols]]
        for s, m in CORNER_SIDES[c]:
            own_cols = slice(s * elems, (s + 1) * elems)
            end = jnp.where(flip[:, own_cols] == 1, 1 - m // 3, m // 3)
            codes.append(corner_source(slot_c[:, own_cols], end, local[:, own_cols]))
        weights.append(rows_hot(sides, *codes))
    corners = jnp.concatenate([x_ref[p] for p in CORNER_POINTS], axis=1)
    lhs = jnp.concatenate([split(corners), corner_far], axis=0)
    for c in range(4):
        cols = slice(c * elems, (c + 1) * elems)
        got = dot_nn(lhs, weights[c])
        xd_ref[CORNER_POINTS[c]] = corners[:, cols] + got[:fields] + got[fields : 2 * fields]
        far_ref[c] = corner_far[:, cols] + got[2 * fields :].astype(BF16)
    inner = []
    for m in (1, 2):
        inner.append(split(jnp.concatenate([x_ref[SIDE_POINTS[s][m]] for s in range(4)], axis=1)))
    inner = jnp.concatenate(inner, axis=0)
    for s in range(4):
        cols = slice(s * elems, (s + 1) * elems)
        got = dot_nn(inner, rows_hot(sides, near[:, cols]))
        one = got[:fields] + got[fields : 2 * fields]
        two = got[2 * fields : 3 * fields] + got[3 * fields :]
        turned = flip[:, cols] == 1
        for m, mine, swapped in ((1, one, two), (2, two, one)):
            p = SIDE_POINTS[s][m]
            xd_ref[p] = x_ref[p] + jnp.where(turned, swapped, mine)
    for p in (5, 6, 9, 10):
        xd_ref[p] = x_ref[p]

    weight = sph_ref[...] * inv_ref[...]
    levels = rden_ref.shape[0]
    for c in range(4):
        cols = slice(c * elems, (c + 1) * elems)
        mix, far_mix = None, None
        for k in range(16):
            if 2 * (k // 8) + k % 4 // 2 != c:
                continue
            wk = weight[k : k + 1, :]
            term = xd_ref[k] * wk
            mix = term if mix is None else mix + term
            if k in POINT_NUMBER:
                term = far_ref[POINT_NUMBER[k]].astype(F32) * wk
                far_mix = term if far_mix is None else far_mix + term
        mix_ref[:, cols] = mix * jnp.concatenate([rden_ref[:, cols]] * (fields // levels), axis=0)
        high = far_mix.astype(BF16)
        far_mix_ref[:256, cols] = high
        far_mix_ref[256:512, cols] = high
        far_mix_ref[512:, cols] = (far_mix - high.astype(F32)).astype(BF16)


def pack(odd, msg):
    half = msg.shape[0] // 2
    low = iota((half, 128), 1) < 64
    top, bottom = msg[:half], msg[half:]
    above = jnp.where(low, top, pltpu.roll(bottom, 64, 1))
    below = jnp.where(low, pltpu.roll(top, 64, 1), bottom)
    return jnp.where(odd == 1, below, above), jnp.where(odd == 1, above, below)


def merge(odd, a, b):
    low = iota(a.shape, 1) < 64
    lower = jnp.where(odd == 1, a, b)
    upper = jnp.where(odd == 1, b, a)
    top = jnp.where(low, lower, pltpu.roll(upper, 64, 1))
    bottom = jnp.where(low, pltpu.roll(lower, 64, 1), upper)
    return jnp.concatenate([top, bottom], axis=0)


def middle_kernel(odd_ref, row_odd_ref, a_ref, b_ref, two_ref, mid_ref, held_ref, got_ref, out_a_ref, out_b_ref):
    got = merge(odd_ref[0], a_ref[...], b_ref[...])
    got_ref[...] = got
    fields = got.shape[0]
    add = dot_nn(split(got), mid_ref[...])
    msg = two_ref[...] + add[:fields] + add[fields:]
    out_a_ref[...], out_b_ref[...] = pack(row_odd_ref[0], msg)


def send_kernel(odd_ref, one_ref, a_ref, b_ref, far_mix_ref, mix_ref, rden_ref, key_ref, rows_ref, held_ref, far_held_ref, two_ref, out_ref):
    fields = mix_ref.shape[0]
    levels = rden_ref.shape[0]
    two = merge(odd_ref[0], a_ref[...], b_ref[...])
    two_ref[...] = two
    got = split(jnp.concatenate([one_ref[...], two], axis=1), axis=1)
    add = dot_nn(jnp.concatenate([got, got[:, :256]], axis=1), far_mix_ref[...])
    mix_hl = split(mix_ref[...] + add * jnp.concatenate([rden_ref[...]] * (fields // levels), axis=0))
    peers = rows_ref.shape[1]
    chunk = 512
    key = key_ref[:1, :]
    for block in range(peers * 8 // chunk):
        res = dot_nt(rows_hot(chunk, key - block * chunk), mix_hl)
        res = res[:, :fields] + res[:, fields:]
        for d in range(chunk // 8):
            row = (block * (chunk // 8) + d) * ROWS
            out_ref[row : row + 8, :] = res[d * 8 : d * 8 + 8, :]
    out_ref[pl.ds(8, peers, stride=ROWS), :] = rows_ref[0]
    out_ref[pl.ds(9, peers, stride=ROWS), :] = rows_ref[1]


def mass_kernel(xd_ref, one_ref, two_ref, far_ref, inv_ref, tm_ref, frame_ref):
    @pl.when(pl.program_id(0) == 0)
    def _():
        total = frame_ref.shape[0]
        row, lane = iota((total, 128), 0), iota((total, 128), 1)
        source = row // ROWS
        frame_ref[:, :128] = hot(lane == source)
        frame_ref[:, 128:] = hot(lane // 16 == row - ROWS * source)

    fields = xd_ref.shape[1]
    got = split(jnp.concatenate([one_ref[...], two_ref[...]], axis=1))
    for k in range(16):
        value = xd_ref[k]
        if k in POINT_NUMBER:
            far = dot_nn(got, far_ref[POINT_NUMBER[k]])
            value = value + far[:fields] + far[fields:]
        tm_ref[pl.ds(k, fields, stride=16), :] = value * inv_ref[k : k + 1, :]


def gathered(buf_ref, pick_ref, meta_ref, levels):
    total = buf_ref.shape[0]
    peers = total // ROWS
    slots = pick_ref.shape[0]
    meta = meta_ref[...]
    thick = dot_nn(meta[:, :128], split(buf_ref[pl.ds(8, peers, stride=ROWS), :], axis=1))
    thick = (thick[:, :128] + thick[:, 128:]) * meta[:, 128:].astype(F32)
    row, lane = iota((384, 128), 0), iota((384, 128), 1)
    fold = hot(jnp.where(row < 256, row % levels, levels) == lane)
    narrow = dot_nn(jnp.concatenate([split(thick, axis=1), meta[:, :128]], axis=1), fold)
    stack = split(buf_ref[...], axis=1)
    outs = []
    for block in range(slots // 128):
        rows = slice(block * 128, (block + 1) * 128)
        got = dot_nn(pick_ref[rows, :], stack)
        outs.append(jnp.concatenate([jnp.transpose(got[:, :128] + got[:, 128:]), jnp.transpose(narrow[rows])], axis=0))
    return outs


def place_kernel(lev_ref, own_ref, frame_ref, pick_ref, meta_ref, half_ref, *, levels):
    total = own_ref.shape[0]
    peers = total // ROWS
    slots = pick_ref.shape[0]
    ids = own_ref[pl.ds(9, peers, stride=ROWS), :]
    ids_t = jnp.transpose(ids)[:16, :]
    cand = dot_nt(split(ids_t), frame_ref[:, :128])
    cand = cand[:16] + cand[16:]
    spot = iota((16, total), 1) % ROWS
    key = jnp.sum(jnp.where((spot == iota((16, total), 0)) & (spot < 8), cand, 0.0), axis=0, keepdims=True)
    key = jnp.where(iota((1, total), 1) % ROWS < 8, key, -9999.0).astype(jnp.int32)
    key = key - lev_ref[0] * slots
    for block in range(slots // 128):
        rows = slice(block * 128, (block + 1) * 128)
        pick_ref[rows, :] = rows_hot(128, key - block * 128)
        meta_ref[rows, :] = dot_nn(pick_ref[rows, :], frame_ref[...]).astype(BF16)
    for block, got in enumerate(gathered(own_ref, pick_ref, meta_ref, levels)):
        half_ref[:, block * 128 : (block + 1) * 128] = got


def physics_kernel(lev_ref, half_ref, par_ref, pick_ref, meta_ref, mix_ref, sig_ref):
    lev = lev_ref[0]
    levels2 = sig_ref.shape[0]
    fields = par_ref.shape[1]
    levels = levels2 // 2
    tracers = fields // levels
    for block, other in enumerate(gathered(par_ref, pick_ref, meta_ref, levels)):
        cols = slice(block * 128, (block + 1) * 128)
        mine = half_ref[:, cols]
        first = jnp.where(lev == 0, mine, other)
        last = jnp.where(lev == 0, other, mine)
        thick = jnp.concatenate([first[fields : fields + levels], last[fields : fields + levels]], axis=0)
        live = first[fields + levels : fields + levels + 1]
        running = jnp.zeros_like(live)
        above = []
        for level in range(levels2):
            above.append(running)
            running = running + thick[level : level + 1]
        above = jnp.concatenate(above, axis=0)
        scale = live / (TOP_PRESSURE + running)
        sigma = (TOP_PRESSURE + above + 0.5 * thick) * scale
        sig_ref[:, cols] = sigma
        share = 1.0 / (running + 1.0 - live)
        for t in range(tracers):
            mix = jnp.concatenate([first[t * levels : (t + 1) * levels], last[t * levels : (t + 1) * levels]], axis=0)
            mean = jnp.sum(thick * mix, axis=0, keepdims=True) * share
            mix_ref[t * levels2 : (t + 1) * levels2, cols] = mix + MIXING_RATE * sigma * (mean - mix)


def halved(shape):
    lead = (0,) * (len(shape) - 1)
    return pl.BlockSpec(shape[:-1] + (shape[-1] // 2,), lambda i: lead + (i,))


def call(kernel, outs, ins, hbm=(), held=(), scratch=(), vmem=16):
    specs = []
    for number, value in enumerate(ins):
        space = pltpu.SMEM if value.shape == (1,) else pltpu.HBM if number in hbm else pltpu.VMEM
        space = pl.ANY if number in held else space
        specs.append(pl.BlockSpec(memory_space=space))
    ins = [pltpu.with_memory_space_constraint(x, pltpu.HBM) if n in hbm else x for n, x in enumerate(ins)]
    return pl.pallas_call(
        kernel,
        out_shape=[out[2](*out[:2]) if len(out) > 2 else jax.ShapeDtypeStruct(*out) for out in outs],
        in_specs=specs,
        out_specs=[pl.BlockSpec(memory_space=out[2] if len(out) > 2 else pltpu.VMEM) for out in outs],
        scratch_shapes=list(scratch),
        compiler_params=pltpu.CompilerParams(vmem_limit_bytes=vmem * 1024 * 1024),
    )(*ins)


def swap(value, step, parity, count, row=None):
    pairs = []
    for i in range(count - step):
        if i // step % 2 == parity and (row is None or i // row == (i + step) // row):
            pairs += [(i, i + step), (i + step, i)]
    return lax.ppermute(value, "sfc", pairs)


def body(
    tracers,
    layer_mass,
    layer_mass_next,
    wind,
    spheremp,
    inverse_mass,
    rec_peer,
    rec_slot,
    rec_flip,
    publish_list,
    column_slot_table,
):
    own_index = lax.axis_index("sfc").astype(jnp.int32)
    lev_index = lax.axis_index("lev").astype(jnp.int32)
    sfc_count = lax.axis_size("sfc")
    lev_count = lax.axis_size("lev")
    tracer_count, level_count, points, elems = tracers.shape
    fields = tracer_count * level_count
    block_cols = sfc_count // DEV_ROWS
    own = own_index.reshape(1)
    col_odd = (own_index % block_cols % 2).reshape(1)
    row_odd = (own_index // block_cols % 2).reshape(1)

    rows = level_count * points
    half = elems // 2
    cols = NPG * elems
    ints = jnp.int32
    ins = [
        own,
        col_odd,
        tracers.reshape(fields * points, elems),
        layer_mass.reshape(rows, elems),
        wind.reshape(2 * rows, elems),
        spheremp,
        rec_peer,
        rec_slot,
        rec_flip,
        publish_list.reshape(1, -1),
        column_slot_table,
        layer_mass_next.reshape(rows, elems),
        inverse_mass,
    ]
    weighted, first_a, first_b, second, info, sph, peer, slot, flip, pub, table, after, inv = call(
        functools.partial(flux_kernel, block_cols),
        [
            ((points, fields, elems), F32, pltpu.VMEM),
            ((fields // 2, 128), F32),
            ((fields // 2, 128), F32),
            ((fields, 128), F32),
            ((8, 4 * elems), ints),
            (spheremp.shape, F32),
            (rec_peer.shape, ints),
            (rec_slot.shape, ints),
            (rec_flip.shape, ints),
            ((1, publish_list.shape[0]), ints),
            (column_slot_table.shape, ints),
            ((2, rows, half), F32),
            (inverse_mass.shape, F32),
        ],
        ins,
        hbm=range(2, len(ins)),
        scratch=[
            pltpu.VMEM((2, fields * points, half), F32),
            pltpu.VMEM((2, rows, half), F32),
            pltpu.VMEM((2, 2 * rows, half), F32),
            pltpu.VMEM((3, points, level_count, half), F32),
            pltpu.SemaphoreType.DMA((17,)),
        ],
    )
    near_a = swap(first_a, 1, 0, sfc_count, block_cols)
    near_b = swap(first_b, 1, 1, sfc_count, block_cols)
    group_width = 5 * NPG * elems // 4
    recv, mid, key, rden, extra = call(
        functools.partial(plan_kernel, block_cols, group_width),
        [
            ((8, 4 * elems), ints),
            ((128, 128), BF16),
            ((8, cols), ints),
            ((level_count, cols), F32),
            ((2, sfc_count, 128), F32),
        ],
        [own, peer, flip, pub, info, table, after, sph, weighted],
        held=(8,),
    )
    got_one, second_a, second_b = call(
        middle_kernel,
        [((fields, 128), F32), ((fields // 2, 128), F32), ((fields // 2, 128), F32)],
        [col_odd, row_odd, near_a, near_b, second, mid, weighted],
        held=(6,),
    )
    over_a = swap(second_a, block_cols, 0, sfc_count)
    over_b = swap(second_b, block_cols, 1, sfc_count)
    weighted, _ = lax.optimization_barrier((weighted, second_a))
    local, far, far_mix, mix = call(
        local_kernel,
        [
            ((points, fields, elems), F32, pltpu.VMEM),
            ((12, 256, elems), BF16, pltpu.VMEM),
            ((768, cols), BF16),
            ((fields, cols), F32),
        ],
        [own, weighted, peer, slot, flip, recv, sph, inv, rden],
    )
    got_two, send = call(
        send_kernel,
        [((fields, 128), F32), ((ROWS * sfc_count, fields), F32)],
        [row_odd, got_one, over_a, over_b, far_mix, mix, rden, key, extra, local, far],
        held=(9, 10),
    )
    moved = lax.all_to_all(
        send.reshape(sfc_count, 1, ROWS * fields), "sfc", split_axis=0, concat_axis=0, tiled=True
    ).reshape(ROWS * sfc_count, fields)
    whole = pl.BlockSpec((fields, 128), lambda i: (0, 0))
    mass, frame = pl.pallas_call(
        mass_kernel,
        grid=(2,),
        out_shape=[
            jax.ShapeDtypeStruct((fields * points, elems), F32),
            jax.ShapeDtypeStruct((ROWS * sfc_count, 256), BF16),
        ],
        in_specs=[halved(local.shape), whole, whole, halved(far.shape), halved(inv.shape)],
        out_specs=[halved((fields * points, elems)), pl.BlockSpec((ROWS * sfc_count, 256), lambda i: (0, 0))],
        compiler_params=pltpu.CompilerParams(vmem_limit_bytes=12 * 1024 * 1024),
        cost_estimate=pl.CostEstimate(flops=2 * 256 * 256 * 3072, bytes_accessed=16 * fields * points * elems, transcendentals=0),
    )(local, got_one, got_two, far, inv)
    moved, mass, frame = lax.optimization_barrier((moved, mass, frame))
    other = lax.ppermute(moved, "lev", [(0, 1), (1, 0)])
    slots = group_width // lev_count
    levels = level_count * lev_count
    lev = lev_index.reshape(1)
    pick, meta, own_half = call(
        functools.partial(place_kernel, levels=level_count),
        [((slots, ROWS * sfc_count), BF16), ((slots, 256), BF16), ((fields + 128, slots), F32)],
        [lev, moved, frame],
    )
    mixed, sigma = call(
        physics_kernel,
        [((tracer_count * levels, slots), F32), ((levels, slots), F32)],
        [lev, own_half, other, pick, meta],
    )
    return (
        mass.reshape(tracers.shape),
        mixed.reshape(tracer_count, levels, slots),
        sigma,
    )


def solution(mesh):
    in_specs = (
        P(None, "lev", None, "sfc"),
        P("lev", None, "sfc"),
        P("lev", None, "sfc"),
        P(None, "lev", None, "sfc"),
        P(None, "sfc"),
        P(None, "sfc"),
        P(None, "sfc"),
        P(None, "sfc"),
        P(None, "sfc"),
        P("sfc"),
        P(None, "sfc"),
    )
    out_specs = (
        P(None, "lev", None, "sfc"),
        P(None, None, ("sfc", "lev")),
        P(None, ("sfc", "lev")),
    )
    return jax.shard_map(body, mesh=mesh, in_specs=in_specs, out_specs=out_specs, check_vma=False)
```

```python
import functools

import jax
import jax.numpy as jnp
import numpy as np
from jax import lax
from jax.experimental import pallas as pl
from jax.experimental.pallas import tpu as pltpu
from jax.sharding import PartitionSpec as P

F32 = jnp.float32
BF16 = jnp.bfloat16
NPG = 4
DEV_ROWS = 4
SIDE_POINTS = [[0, 1, 2, 3], [3, 7, 11, 15], [12, 13, 14, 15], [0, 4, 8, 12]]
CORNER_POINTS = [0, 3, 12, 15]
CORNER_SIDES = [[(0, 0), (3, 0)], [(0, 3), (1, 0)], [(2, 0), (3, 3)], [(1, 3), (2, 3)]]
EDGE_SLOTS = [(s, m) for s in range(4) for m in (1, 2)]
POINT_NUMBER = {p: c for c, p in enumerate(CORNER_POINTS)}
POINT_NUMBER.update({SIDE_POINTS[s][m]: 4 + n for n, (s, m) in enumerate(EDGE_SLOTS)})
TIME_STEP = 0.05
TOP_PRESSURE = 1.0
MIXING_RATE = 0.8
PER_SIDE = 16
ROWS = 10


def lagrange_derivative():
    gll_points = np.array([-1.0, -1.0 / np.sqrt(5.0), 1.0 / np.sqrt(5.0), 1.0])
    barycentric = np.array(
        [
            1.0
            / np.prod(
                [gll_points[source] - gll_points[middle] for middle in range(4) if middle != source]
            )
            for source in range(4)
        ]
    )
    derivative = np.zeros((4, 4))
    for target in range(4):
        for source in range(4):
            if target != source:
                derivative[target, source] = (
                    barycentric[source]
                    / barycentric[target]
                    / (gll_points[target] - gll_points[source])
                )
        derivative[target, target] = -np.sum(derivative[target])
    return derivative


def iota(shape, dim):
    return lax.broadcasted_iota(jnp.int32, shape, dim)


def hot(mask):
    return jnp.where(mask, 1.0, 0.0).astype(BF16)


def rows_hot(count, *codes):
    row = lax.broadcasted_iota(jnp.int16, (count, codes[0].shape[1]), 0)
    mask = None
    for code in codes:
        here = row == code.astype(jnp.int16)
        mask = here if mask is None else mask | here
    return jnp.where(mask, jnp.ones((), BF16), jnp.zeros((), BF16))


def split(x, axis=0):
    high = x.astype(BF16)
    low = (x - high.astype(F32)).astype(BF16)
    return jnp.concatenate([high, low], axis=axis)


def dot_nn(a, b):
    return lax.dot_general(a, b, (((1,), (0,)), ((), ())), preferred_element_type=F32)


def dot_nt(a, b):
    return lax.dot_general(a, b, (((1,), (1,)), ((), ())), preferred_element_type=F32)


def wide(ref, first=0):
    return jnp.concatenate([ref[first + s : first + s + 1, :] for s in range(4)], axis=1)


def facing(peer, own, block_cols):
    ahead = peer - own
    code = jnp.full_like(peer, -1)
    for number, offset in enumerate((1, -1, block_cols, -block_cols)):
        code = jnp.where(ahead == offset, number, code)
    return jnp.where(peer >= 0, code, -1)


def ranks(direction, entry):
    count = direction.shape[1]
    code = jnp.where(direction >= 0, direction * 64 + entry, -1)
    found = jnp.where(iota((256, count), 0) == code, 1.0, 0.0)
    present = jnp.max(found, axis=1, keepdims=True)
    row, col = iota((256, 256), 0), iota((256, 256), 1)
    before = hot((col < row) & (col // 64 == row // 64))
    below = dot_nn(before, jnp.broadcast_to(present, (256, 128)).astype(BF16))
    rank = jnp.sum(found * below[:, :1], axis=0, keepdims=True)
    return rank.astype(jnp.int32)


def flux_kernel(
    block_cols, own_ref, odd_ref, tr_hbm, lm_hbm, wd_hbm, sph_hbm, peer_hbm, slot_hbm, flip_hbm, pub_hbm, table_hbm, next_hbm, inv_hbm,
    x_ref, one_a_ref, one_b_ref, two_ref, info_ref, sph_ref, peer_ref, slot_ref, flip_ref, pub_ref, table_ref, next_ref, inv_ref,
    tr_ref, lm_ref, wd_ref, flow_ref, sems
):
    deriv = lagrange_derivative() * TIME_STEP
    levels = lm_ref.shape[1] // 16
    tracers = tr_ref.shape[1] // lm_ref.shape[1]
    elems = peer_ref.shape[1]
    lanes = tr_ref.shape[2]
    copies = []

    def fetch(src, dst):
        copy = pltpu.make_async_copy(src, dst, sems.at[len(copies)])
        copy.start()
        copies.append(copy)
        return copy

    small = [fetch(peer_hbm, peer_ref), fetch(slot_hbm, slot_ref), fetch(sph_hbm, sph_ref)]
    big = []
    for half in range(2):
        cut = slice(half * lanes, (half + 1) * lanes)
        big.append(
            [
                fetch(lm_hbm.at[:, cut], lm_ref.at[half]),
                fetch(wd_hbm.at[:, cut], wd_ref.at[half]),
            ]
        )
        for part in range(2):
            rows = pl.ds(part * (tr_ref.shape[1] // 2), tr_ref.shape[1] // 2)
            big[half].append(fetch(tr_hbm.at[rows, cut], tr_ref.at[half, rows]))
    for copy in small:
        copy.wait()
    direction = facing(wide(peer_ref), own_ref[0], block_cols)
    rank = ranks(direction, jnp.clip(wide(slot_ref), 0, 63))
    usable = (direction >= 0) & (rank < PER_SIDE)
    base = jnp.where(usable, direction * 64 + rank, -1000)
    info_ref[...] = jnp.broadcast_to(base, info_ref.shape)
    later = [fetch(flip_hbm, flip_ref), fetch(pub_hbm, pub_ref), fetch(table_hbm, table_ref), fetch(inv_hbm, inv_ref)]
    for half in range(2):
        later.append(fetch(next_hbm.at[:, half * lanes : (half + 1) * lanes], next_ref.at[half]))

    for half in range(2):
        cut = slice(half * lanes, (half + 1) * lanes)
        for copy in big[half][:2]:
            copy.wait()
        tr_half, lm_half, wd_half = tr_ref.at[half], lm_ref.at[half], wd_ref.at[half]
        for k in range(16):
            flow_ref[0, k] = lm_half[pl.ds(k, levels, stride=16), :]
            flow_ref[1, k] = wd_half[pl.ds(k, levels, stride=16), :]
            flow_ref[2, k] = wd_half[pl.ds(levels * 16 + k, levels, stride=16), :]

        def one(t, carry):
            mass, fa, fb = [], [], []
            for k in range(16):
                tr = tr_half[pl.ds(t * (levels * 16) + k, levels, stride=16), :]
                mk = tr * flow_ref[0, k]
                mass.append(mk)
                fa.append(mk * flow_ref[1, k])
                fb.append(mk * flow_ref[2, k])
            for k in range(16):
                j, i = k // 4, k % 4
                value = mass[k]
                for other in range(4):
                    if abs(deriv[i, other]) > 1e-12:
                        value = value - deriv[i, other] * fa[4 * j + other]
                    if abs(deriv[j, other]) > 1e-12:
                        value = value - deriv[j, other] * fb[4 * other + i]
                x_ref[k, pl.ds(pl.multiple_of(t * levels, levels), levels), cut] = value * sph_ref[k : k + 1, cut]
            return carry

        for part in range(2):
            big[half][2 + part].wait()
            lax.fori_loop(part * (tracers // 2), (part + 1) * (tracers // 2), one, 0)

    total = None
    for group in [[pair] for pair in EDGE_SLOTS] + CORNER_SIDES:
        pick = rows_hot(256, *[base[:, s * elems : (s + 1) * elems] + m * PER_SIDE for s, m in group])
        s, m = group[0]
        part = dot_nt(split(x_ref[SIDE_POINTS[s][m]]), pick)
        total = part if total is None else total + part
    fields = total.shape[0] // 2
    total = total[:fields] + total[fields:]
    one_a_ref[...], one_b_ref[...] = pack(odd_ref[0], total[:, :128])
    two_ref[...] = total[:, 128:]
    for copy in later:
        copy.wait()


def arrive(recv, turn, elems, s, m):
    cols = slice(s * elems, (s + 1) * elems)
    turned = jnp.where(turn[:, cols] == 1, 3 - m, m)
    return recv[:, cols] + turned * PER_SIDE


def plan_kernel(
    block_cols, group_width, own_ref, peer_ref, flip_ref, pub_ref, info_ref, table_ref, next_ref, sph_ref, held_ref,
    recv_ref, mid_ref, key_ref, rden_ref, rows_ref
):
    elems = peer_ref.shape[1]
    sides = 4 * elems
    peer, flip = wide(peer_ref), wide(flip_ref)
    at = iota((1, sides), 1)
    entries = pub_ref.shape[1]
    square = iota((entries, entries), 0) == iota((entries, entries), 1)
    listed = jnp.sum(jnp.where(square, pub_ref[...].astype(F32), 0.0), axis=1, keepdims=True).astype(jnp.int32)
    own_code = 4 * (at % elems) + at // elems
    match = jnp.where(listed == own_code, 1.0, 0.0)
    place = jnp.sum(match * iota((entries, sides), 0).astype(F32), axis=0, keepdims=True).astype(jnp.int32)
    direction = facing(peer, own_ref[0], block_cols)
    rank = ranks(direction, place)
    usable = (direction >= 0) & (rank < PER_SIDE)
    start = jnp.where(direction == 0, 64, jnp.where(direction == 1, 0, jnp.where(direction == 2, 192, 128)))
    recv = jnp.where(usable, start + rank, -1000)
    recv_ref[...] = jnp.broadcast_to(recv, recv_ref.shape)
    base = info_ref[:1, :]
    second = jnp.where(base >= 128, base - 128, -1000)
    sent, got = [], []
    for c in range(4):
        got.append(rows_hot(128, *[arrive(recv, flip, elems, s, m) for s, m in CORNER_SIDES[c]]))
        sent.append(rows_hot(128, *[second[:, s * elems : (s + 1) * elems] + m * PER_SIDE for s, m in CORNER_SIDES[c]]))
    mid_ref[...] = dot_nt(jnp.concatenate(got, axis=1), jnp.concatenate(sent, axis=1)).astype(BF16)

    levels = next_ref.shape[1] // 16
    sph = sph_ref[...]
    thicks = []
    for c in range(4):
        den, area = None, None
        for k in range(16):
            if 2 * (k // 8) + k % 4 // 2 != c:
                continue
            weight = sph[k : k + 1, :]
            term = [next_ref.at[half][pl.ds(k, levels, stride=16), :] for half in range(2)]
            term = jnp.concatenate(term, axis=1) * weight
            den = term if den is None else den + term
            area = weight if area is None else area + weight
        rden_ref[:, c * elems : (c + 1) * elems] = 1.0 / den
        thicks.append(den / area)
    thick = jnp.concatenate(thicks, axis=1)
    total = 4 * elems
    slot = wide(table_ref)
    slot_f = slot.astype(F32)
    dest = jnp.floor((slot_f + 0.5) * (1.0 / group_width)).astype(jnp.int32)
    within = (slot - dest * group_width).astype(F32)
    peers = rows_ref.shape[1]
    to = jnp.where(iota((peers, total), 0) == dest, 1.0, 0.0)
    to_b = to.astype(BF16)
    upto = hot(iota((128, 128), 0) < iota((128, 128), 1))
    before = jnp.zeros((peers, 1), F32)
    parts = []
    for block in range(total // 128):
        cols = slice(block * 128, block * 128 + 128)
        parts.append(dot_nn(to_b[:, cols], upto) + before)
        before = before + jnp.sum(to[:, cols], axis=1, keepdims=True)
    rank = jnp.sum(to * jnp.concatenate(parts, axis=1), axis=0, keepdims=True).astype(jnp.int32)
    key = dest * 8 + rank
    key_ref[...] = jnp.broadcast_to(key, key_ref.shape)
    at = iota((128, total), 0)
    spread = jnp.where(at // levels == rank, jnp.concatenate([thick] * (128 // levels), axis=0), 0.0)
    ids = jnp.where(at == rank, within, 0.0)
    both = jnp.concatenate([split(spread), split(ids)], axis=0)
    got = dot_nt(to_b, both)
    rows_ref[0] = got[:, :128] + got[:, 128:256]
    rows_ref[1] = got[:, 256:384] + got[:, 384:]


def local_kernel(
    own_ref, x_ref, peer_ref, slot_ref, flip_ref, recv_ref, sph_ref, inv_ref, rden_ref, xd_ref, far_ref, far_mix_ref, mix_ref
):
    own = own_ref[0]
    elems = peer_ref.shape[1]
    fields = x_ref.shape[1]
    sides = 4 * elems
    peer, slot, flip = wide(peer_ref), wide(slot_ref), wide(flip_ref)
    recv = recv_ref[:1, :]
    corner_far = []
    for c in range(4):
        corner_far.append(rows_hot(256, *[arrive(recv, flip, elems, s, m) for s, m in CORNER_SIDES[c]]))
    corner_far = jnp.concatenate(corner_far, axis=1)
    for number, (s, m) in enumerate(EDGE_SLOTS):
        far_ref[4 + number] = rows_hot(256, arrive(recv, flip, elems, s, m))

    local = peer == own
    slot_c = jnp.clip(slot, 0, 4 * elems - 1)
    near = jnp.where(local, slot_c % 4 * elems + slot_c // 4, -1)

    def corner_source(code, end, ok):
        side = code % 4
        corner = jnp.where(side == 1, 1, jnp.where(side == 2, 2, 0)) + end * jnp.where(side % 2 == 1, 2, 1)
        return jnp.where(ok, corner * elems + code // 4, -1)

    cpeer, cslot, cflip = wide(peer_ref, 4), wide(slot_ref, 4), wide(flip_ref, 4)
    third = corner_source(jnp.clip(cslot, 0, 4 * elems - 1), cflip, cpeer == own)
    weights = []
    for c in range(4):
        cols = slice(c * elems, (c + 1) * elems)
        codes = [third[:, cols]]
        for s, m in CORNER_SIDES[c]:
            own_cols = slice(s * elems, (s + 1) * elems)
            end = jnp.where(flip[:, own_cols] == 1, 1 - m // 3, m // 3)
            codes.append(corner_source(slot_c[:, own_cols], end, local[:, own_cols]))
        weights.append(rows_hot(sides, *codes))
    corners = jnp.concatenate([x_ref[p] for p in CORNER_POINTS], axis=1)
    lhs = jnp.concatenate([split(corners), corner_far], axis=0)
    for c in range(4):
        cols = slice(c * elems, (c + 1) * elems)
        got = dot_nn(lhs, weights[c])
        xd_ref[CORNER_POINTS[c]] = corners[:, cols] + got[:fields] + got[fields : 2 * fields]
        far_ref[c] = corner_far[:, cols] + got[2 * fields :].astype(BF16)
    inner = []
    for m in (1, 2):
        inner.append(split(jnp.concatenate([x_ref[SIDE_POINTS[s][m]] for s in range(4)], axis=1)))
    inner = jnp.concatenate(inner, axis=0)
    for s in range(4):
        cols = slice(s * elems, (s + 1) * elems)
        got = dot_nn(inner, rows_hot(sides, near[:, cols]))
        one = got[:fields] + got[fields : 2 * fields]
        two = got[2 * fields : 3 * fields] + got[3 * fields :]
        turned = flip[:, cols] == 1
        for m, mine, swapped in ((1, one, two), (2, two, one)):
            p = SIDE_POINTS[s][m]
            xd_ref[p] = x_ref[p] + jnp.where(turned, swapped, mine)
    for p in (5, 6, 9, 10):
        xd_ref[p] = x_ref[p]

    weight = sph_ref[...] * inv_ref[...]
    levels = rden_ref.shape[0]
    for c in range(4):
        cols = slice(c * elems, (c + 1) * elems)
        mix, far_mix = None, None
        for k in range(16):
            if 2 * (k // 8) + k % 4 // 2 != c:
                continue
            wk = weight[k : k + 1, :]
            term = xd_ref[k] * wk
            mix = term if mix is None else mix + term
            if k in POINT_NUMBER:
                term = far_ref[POINT_NUMBER[k]].astype(F32) * wk
                far_mix = term if far_mix is None else far_mix + term
        mix_ref[:, cols] = mix * jnp.concatenate([rden_ref[:, cols]] * (fields // levels), axis=0)
        high = far_mix.astype(BF16)
        far_mix_ref[:256, cols] = high
        far_mix_ref[256:512, cols] = high
        far_mix_ref[512:, cols] = (far_mix - high.astype(F32)).astype(BF16)


def pack(odd, msg):
    half = msg.shape[0] // 2
    low = iota((half, 128), 1) < 64
    top, bottom = msg[:half], msg[half:]
    above = jnp.where(low, top, pltpu.roll(bottom, 64, 1))
    below = jnp.where(low, pltpu.roll(top, 64, 1), bottom)
    return jnp.where(odd == 1, below, above), jnp.where(odd == 1, above, below)


def merge(odd, a, b):
    low = iota(a.shape, 1) < 64
    lower = jnp.where(odd == 1, a, b)
    upper = jnp.where(odd == 1, b, a)
    top = jnp.where(low, lower, pltpu.roll(upper, 64, 1))
    bottom = jnp.where(low, pltpu.roll(lower, 64, 1), upper)
    return jnp.concatenate([top, bottom], axis=0)


def middle_kernel(odd_ref, row_odd_ref, a_ref, b_ref, two_ref, mid_ref, held_ref, got_ref, out_a_ref, out_b_ref):
    got = merge(odd_ref[0], a_ref[...], b_ref[...])
    got_ref[...] = got
    fields = got.shape[0]
    add = dot_nn(split(got), mid_ref[...])
    msg = two_ref[...] + add[:fields] + add[fields:]
    out_a_ref[...], out_b_ref[...] = pack(row_odd_ref[0], msg)


def send_kernel(odd_ref, one_ref, a_ref, b_ref, far_mix_ref, mix_ref, rden_ref, key_ref, rows_ref, held_ref, far_held_ref, two_ref, out_ref):
    fields = mix_ref.shape[0]
    levels = rden_ref.shape[0]
    two = merge(odd_ref[0], a_ref[...], b_ref[...])
    two_ref[...] = two
    got = split(jnp.concatenate([one_ref[...], two], axis=1), axis=1)
    add = dot_nn(jnp.concatenate([got, got[:, :256]], axis=1), far_mix_ref[...])
    mix_hl = split(mix_ref[...] + add * jnp.concatenate([rden_ref[...]] * (fields // levels), axis=0))
    peers = rows_ref.shape[1]
    chunk = 512
    key = key_ref[:1, :]
    for block in range(peers * 8 // chunk):
        res = dot_nt(rows_hot(chunk, key - block * chunk), mix_hl)
        res = res[:, :fields] + res[:, fields:]
        for d in range(chunk // 8):
            row = (block * (chunk // 8) + d) * ROWS
            out_ref[row : row + 8, :] = res[d * 8 : d * 8 + 8, :]
    out_ref[pl.ds(8, peers, stride=ROWS), :] = rows_ref[0]
    out_ref[pl.ds(9, peers, stride=ROWS), :] = rows_ref[1]


def mass_kernel(xd_ref, one_ref, two_ref, far_ref, inv_ref, tm_ref, frame_ref):
    @pl.when(pl.program_id(0) == 0)
    def _():
        total = frame_ref.shape[0]
        row, lane = iota((total, 128), 0), iota((total, 128), 1)
        source = row // ROWS
        frame_ref[:, :128] = hot(lane == source)
        frame_ref[:, 128:] = hot(lane // 16 == row - ROWS * source)

    fields = xd_ref.shape[1]
    got = split(jnp.concatenate([one_ref[...], two_ref[...]], axis=1))
    for k in range(16):
        value = xd_ref[k]
        if k in POINT_NUMBER:
            far = dot_nn(got, far_ref[POINT_NUMBER[k]])
            value = value + far[:fields] + far[fields:]
        tm_ref[pl.ds(k, fields, stride=16), :] = value * inv_ref[k : k + 1, :]


def gathered(buf_ref, pick_ref, meta_ref, levels):
    total = buf_ref.shape[0]
    peers = total // ROWS
    slots = pick_ref.shape[0]
    meta = meta_ref[...]
    thick = dot_nn(meta[:, :128], split(buf_ref[pl.ds(8, peers, stride=ROWS), :], axis=1))
    thick = (thick[:, :128] + thick[:, 128:]) * meta[:, 128:].astype(F32)
    row, lane = iota((384, 128), 0), iota((384, 128), 1)
    fold = hot(jnp.where(row < 256, row % levels, levels) == lane)
    narrow = dot_nn(jnp.concatenate([split(thick, axis=1), meta[:, :128]], axis=1), fold)
    stack = split(buf_ref[...], axis=1)
    outs = []
    for block in range(slots // 128):
        rows = slice(block * 128, (block + 1) * 128)
        got = dot_nn(pick_ref[rows, :], stack)
        outs.append(jnp.concatenate([jnp.transpose(got[:, :128] + got[:, 128:]), jnp.transpose(narrow[rows])], axis=0))
    return outs


def place_kernel(lev_ref, own_ref, frame_ref, pick_ref, meta_ref, half_ref, *, levels):
    total = own_ref.shape[0]
    peers = total // ROWS
    slots = pick_ref.shape[0]
    ids = own_ref[pl.ds(9, peers, stride=ROWS), :]
    ids_t = jnp.transpose(ids)[:16, :]
    cand = dot_nt(split(ids_t), frame_ref[:, :128])
    cand = cand[:16] + cand[16:]
    spot = iota((16, total), 1) % ROWS
    key = jnp.sum(jnp.where((spot == iota((16, total), 0)) & (spot < 8), cand, 0.0), axis=0, keepdims=True)
    key = jnp.where(iota((1, total), 1) % ROWS < 8, key, -9999.0).astype(jnp.int32)
    key = key - lev_ref[0] * slots
    for block in range(slots // 128):
        rows = slice(block * 128, (block + 1) * 128)
        pick_ref[rows, :] = rows_hot(128, key - block * 128)
        meta_ref[rows, :] = dot_nn(pick_ref[rows, :], frame_ref[...]).astype(BF16)
    for block, got in enumerate(gathered(own_ref, pick_ref, meta_ref, levels)):
        half_ref[:, block * 128 : (block + 1) * 128] = got


def physics_kernel(lev_ref, half_ref, par_ref, pick_ref, meta_ref, mix_hbm, sig_hbm, mix_ref, sig_ref, sems):
    lev = lev_ref[0]
    copies = []
    levels2 = sig_ref.shape[0]
    fields = par_ref.shape[1]
    levels = levels2 // 2
    tracers = fields // levels
    for block, other in enumerate(gathered(par_ref, pick_ref, meta_ref, levels)):
        cols = slice(block * 128, (block + 1) * 128)
        mine = half_ref[:, cols]
        first = jnp.where(lev == 0, mine, other)
        last = jnp.where(lev == 0, other, mine)
        thick = jnp.concatenate([first[fields : fields + levels], last[fields : fields + levels]], axis=0)
        live = first[fields + levels : fields + levels + 1]
        running = jnp.zeros_like(live)
        above = []
        for level in range(levels2):
            above.append(running)
            running = running + thick[level : level + 1]
        above = jnp.concatenate(above, axis=0)
        scale = live / (TOP_PRESSURE + running)
        sigma = (TOP_PRESSURE + above + 0.5 * thick) * scale
        sig_ref[:, cols] = sigma
        share = 1.0 / (running + 1.0 - live)
        for t in range(tracers):
            mix = jnp.concatenate([first[t * levels : (t + 1) * levels], last[t * levels : (t + 1) * levels]], axis=0)
            mean = jnp.sum(thick * mix, axis=0, keepdims=True) * share
            mix_ref[t * levels2 : (t + 1) * levels2, cols] = mix + MIXING_RATE * sigma * (mean - mix)
        for src, dst in ((mix_ref, mix_hbm), (sig_ref, sig_hbm)):
            copies.append(pltpu.make_async_copy(src.at[:, cols], dst.at[:, cols], sems.at[len(copies)]))
            copies[-1].start()
    for copy in copies:
        copy.wait()


def halved(shape):
    lead = (0,) * (len(shape) - 1)
    return pl.BlockSpec(shape[:-1] + (shape[-1] // 2,), lambda i: lead + (i,))


def call(kernel, outs, ins, hbm=(), held=(), scratch=(), vmem=16):
    specs = []
    for number, value in enumerate(ins):
        space = pltpu.SMEM if value.shape == (1,) else pltpu.HBM if number in hbm else pltpu.VMEM
        space = pl.ANY if number in held else space
        specs.append(pl.BlockSpec(memory_space=space))
    ins = [pltpu.with_memory_space_constraint(x, pltpu.HBM) if n in hbm else x for n, x in enumerate(ins)]
    return pl.pallas_call(
        kernel,
        out_shape=[out[2](*out[:2]) if len(out) > 2 else jax.ShapeDtypeStruct(*out) for out in outs],
        in_specs=specs,
        out_specs=[pl.BlockSpec(memory_space=out[2] if len(out) > 2 else pltpu.VMEM) for out in outs],
        scratch_shapes=list(scratch),
        compiler_params=pltpu.CompilerParams(vmem_limit_bytes=vmem * 1024 * 1024),
    )(*ins)


def swap(value, step, parity, count, row=None):
    pairs = []
    for i in range(count - step):
        if i // step % 2 == parity and (row is None or i // row == (i + step) // row):
            pairs += [(i, i + step), (i + step, i)]
    return lax.ppermute(value, "sfc", pairs)


def body(
    tracers,
    layer_mass,
    layer_mass_next,
    wind,
    spheremp,
    inverse_mass,
    rec_peer,
    rec_slot,
    rec_flip,
    publish_list,
    column_slot_table,
):
    own_index = lax.axis_index("sfc").astype(jnp.int32)
    lev_index = lax.axis_index("lev").astype(jnp.int32)
    sfc_count = lax.axis_size("sfc")
    lev_count = lax.axis_size("lev")
    tracer_count, level_count, points, elems = tracers.shape
    fields = tracer_count * level_count
    block_cols = sfc_count // DEV_ROWS
    own = own_index.reshape(1)
    col_odd = (own_index % block_cols % 2).reshape(1)
    row_odd = (own_index // block_cols % 2).reshape(1)

    rows = level_count * points
    half = elems // 2
    cols = NPG * elems
    ints = jnp.int32
    ins = [
        own,
        col_odd,
        tracers.reshape(fields * points, elems),
        layer_mass.reshape(rows, elems),
        wind.reshape(2 * rows, elems),
        spheremp,
        rec_peer,
        rec_slot,
        rec_flip,
        publish_list.reshape(1, -1),
        column_slot_table,
        layer_mass_next.reshape(rows, elems),
        inverse_mass,
    ]
    weighted, first_a, first_b, second, info, sph, peer, slot, flip, pub, table, after, inv = call(
        functools.partial(flux_kernel, block_cols),
        [
            ((points, fields, elems), F32, pltpu.VMEM),
            ((fields // 2, 128), F32),
            ((fields // 2, 128), F32),
            ((fields, 128), F32),
            ((8, 4 * elems), ints),
            (spheremp.shape, F32),
            (rec_peer.shape, ints),
            (rec_slot.shape, ints),
            (rec_flip.shape, ints),
            ((1, publish_list.shape[0]), ints),
            (column_slot_table.shape, ints),
            ((2, rows, half), F32),
            (inverse_mass.shape, F32),
        ],
        ins,
        hbm=range(2, len(ins)),
        scratch=[
            pltpu.VMEM((2, fields * points, half), F32),
            pltpu.VMEM((2, rows, half), F32),
            pltpu.VMEM((2, 2 * rows, half), F32),
            pltpu.VMEM((3, points, level_count, half), F32),
            pltpu.SemaphoreType.DMA((17,)),
        ],
    )
    near_a = swap(first_a, 1, 0, sfc_count, block_cols)
    near_b = swap(first_b, 1, 1, sfc_count, block_cols)
    group_width = 5 * NPG * elems // 4
    recv, mid, key, rden, extra = call(
        functools.partial(plan_kernel, block_cols, group_width),
        [
            ((8, 4 * elems), ints),
            ((128, 128), BF16),
            ((8, cols), ints),
            ((level_count, cols), F32),
            ((2, sfc_count, 128), F32),
        ],
        [own, peer, flip, pub, info, table, after, sph, weighted],
        held=(8,),
    )
    got_one, second_a, second_b = call(
        middle_kernel,
        [((fields, 128), F32), ((fields // 2, 128), F32), ((fields // 2, 128), F32)],
        [col_odd, row_odd, near_a, near_b, second, mid, weighted],
        held=(6,),
    )
    over_a = swap(second_a, block_cols, 0, sfc_count)
    over_b = swap(second_b, block_cols, 1, sfc_count)
    weighted, _ = lax.optimization_barrier((weighted, second_a))
    local, far, far_mix, mix = call(
        local_kernel,
        [
            ((points, fields, elems), F32, pltpu.VMEM),
            ((12, 256, elems), BF16, pltpu.VMEM),
            ((768, cols), BF16),
            ((fields, cols), F32),
        ],
        [own, weighted, peer, slot, flip, recv, sph, inv, rden],
    )
    got_two, send = call(
        send_kernel,
        [((fields, 128), F32), ((ROWS * sfc_count, fields), F32)],
        [row_odd, got_one, over_a, over_b, far_mix, mix, rden, key, extra, local, far],
        held=(9, 10),
    )
    moved = lax.all_to_all(
        send.reshape(sfc_count, 1, ROWS * fields), "sfc", split_axis=0, concat_axis=0, tiled=True
    ).reshape(ROWS * sfc_count, fields)
    whole = pl.BlockSpec((fields, 128), lambda i: (0, 0))
    mass, frame = pl.pallas_call(
        mass_kernel,
        grid=(2,),
        out_shape=[
            jax.ShapeDtypeStruct((fields * points, elems), F32),
            jax.ShapeDtypeStruct((ROWS * sfc_count, 256), BF16),
        ],
        in_specs=[halved(local.shape), whole, whole, halved(far.shape), halved(inv.shape)],
        out_specs=[halved((fields * points, elems)), pl.BlockSpec((ROWS * sfc_count, 256), lambda i: (0, 0))],
        compiler_params=pltpu.CompilerParams(vmem_limit_bytes=12 * 1024 * 1024),
        cost_estimate=pl.CostEstimate(flops=2 * 256 * 256 * 3072, bytes_accessed=16 * fields * points * elems, transcendentals=0),
    )(local, got_one, got_two, far, inv)
    moved, mass, frame = lax.optimization_barrier((moved, mass, frame))
    other = lax.ppermute(moved, "lev", [(0, 1), (1, 0)])
    slots = group_width // lev_count
    levels = level_count * lev_count
    lev = lev_index.reshape(1)
    pick, meta, own_half = call(
        functools.partial(place_kernel, levels=level_count),
        [((slots, ROWS * sfc_count), BF16), ((slots, 256), BF16), ((fields + 128, slots), F32)],
        [lev, moved, frame],
    )
    mixed, sigma = call(
        physics_kernel,
        [((tracer_count * levels, slots), F32, pltpu.HBM), ((levels, slots), F32, pltpu.HBM)],
        [lev, own_half, other, pick, meta],
        scratch=[
            pltpu.VMEM((tracer_count * levels, slots), F32),
            pltpu.VMEM((levels, slots), F32),
            pltpu.SemaphoreType.DMA((2 * slots // 128,)),
        ],
    )
    return (
        mass.reshape(tracers.shape),
        mixed.reshape(tracer_count, levels, slots),
        sigma,
    )


def solution(mesh):
    in_specs = (
        P(None, "lev", None, "sfc"),
        P("lev", None, "sfc"),
        P("lev", None, "sfc"),
        P(None, "lev", None, "sfc"),
        P(None, "sfc"),
        P(None, "sfc"),
        P(None, "sfc"),
        P(None, "sfc"),
        P(None, "sfc"),
        P("sfc"),
        P(None, "sfc"),
    )
    out_specs = (
        P(None, "lev", None, "sfc"),
        P(None, None, ("sfc", "lev")),
        P(None, ("sfc", "lev")),
    )
    return jax.shard_map(body, mesh=mesh, in_specs=in_specs, out_specs=out_specs, check_vma=False)
```
